512 devices in a mesh: env: 32 (over z, core), sp: 16 (over x, y).
Axes of the slice: x: 4, y: 4, z: 16, core: 2. Of those that a mesh axis runs over, the one named last changes fastest.
Arguments:
- env_desc: bfloat16 [32768, 1000], P('env'), may hold values from -6 to 6
- env_counts: int32 [32, 448], P('env'), may hold values from 1 to 6, 1024 in all within a row
- reg_desc: bfloat16 [2048, 1000], P('env'), may hold values from -6 to 6
- sparse_desc: bfloat16 [80, 256, 1000], P('sp', 'env'), may hold values from -6 to 6
- panel_block: int32 [], replicated, may hold values from 0 to 79
Outputs:
- updated: float32 [16384, 20480], P('env', 'sp')
- coupling: float32 [256, 20480], P(None, 'sp')
The draws below stay inside these ranges and needn't reach their ends.
Inputs may be any that keep to these rules, and one draw needn't show every extreme that they name: Each row of env_counts sums to 1024, and its largest entry is 6.
All inputs are finite; a program needn't handle non-finite values.
Results may differ from the reference program's by a relative error of at most 0.0003.
Values may be sent and summed in bfloat16 or wider, within the bound.
No kernel may reach another device: no remote copies, remote signals or barrier semaphores. Data moves between devices by JAX's collectives and lax.ppermute only.
A program may use at most 64 MiB of HBM per device.

```python
import math
import jax
import jax.numpy as jnp
import numpy as np
from jax import lax

DESC = 1000
M = 20480
PANEL = 256
ENV_DEV = 1024
CONF_DEV = 448
MOST = 6
REG_DEV = 64
ROWS = 16384
ENVS = 32768
REGS = 2048
S_SUB = 256
N_ENV = 32


def level_of(stream_key, extent, shards, smallest, largest):
    gain = 1.0
    for dim, blocks in shards:
        steps = jax.random.uniform(jax.random.fold_in(jax.random.fold_in(stream_key, 6), dim), (blocks,), jnp.float32, smallest / len(shards), largest / len(shards))
        gain = gain * jnp.repeat(jnp.exp(steps), extent[dim] // blocks).reshape((-1,) + (1,) * (len(extent) - 1 - dim))
    return gain


def split_up(count, total, bound, slope):
    loads = [(1 << 20) // math.isqrt(grade ** slope) + 1 for grade in range(2, count + 1)]
    spare, holding = total - bound - (count - 1), [1] * (count - 1)
    while spare > 0:
        movable = [i for i in range(count - 1) if holding[i] < bound]
        pool, left = sum([loads[i] for i in movable]), spare
        for i in movable:
            more = min(bound - holding[i], max(1, left * loads[i] // pool), spare)
            holding[i] = holding[i] + more
            spare = spare - more
    return np.array([bound] + holding)


def uneven(key, amount, total, bound, lean):
    if amount == 2:
        one = jax.random.randint(key, (), max(1, total - bound), min(bound, total - 1) + 1)
        return jnp.stack([one, total - one])
    sizes = jnp.asarray(split_up(amount, total, bound, lean), jnp.int32)
    pairs = (amount - 1) // 2
    source_of, taker = sizes[1:1 + 2 * pairs:2], sizes[2:2 + 2 * pairs:2]
    room = jnp.minimum(source_of - 1, bound - taker)
    passed = jax.random.randint(jax.random.fold_in(key, 1), (pairs,), 0, 1 << 20) % (room + 1)
    sizes = sizes.at[1:1 + 2 * pairs:2].set(source_of - passed).at[2:2 + 2 * pairs:2].set(taker + passed)
    return sizes[jax.random.permutation(jax.random.fold_in(key, 2), amount)]


def bell_draw(stream_key, extent, spread, reach, split=(), kind=jnp.bfloat16):
    entries = jax.random.normal(stream_key, extent, jnp.float32) * spread
    if len(split) > 0:
        entries = level_of(stream_key, extent, split, -0.22, 0.18) * entries
    return jnp.clip(entries, min=-reach, max=reach).astype(kind)


def setup_inputs(seed: int = 0) -> dict:
    streams_of = jax.random.split(jax.random.key(seed), 6)
    env_desc = bell_draw(streams_of[0], (ENVS, DESC), 1.0, 6.0, ((0, 32),))
    env_counts = jax.vmap(lambda own: uneven(own, CONF_DEV, ENV_DEV, MOST, 2))(jax.random.split(streams_of[1], N_ENV)).reshape((N_ENV, CONF_DEV)).astype(jnp.int32)
    reg_desc = bell_draw(streams_of[2], (REGS, DESC), 1.0, 6.0, ((0, 32),))
    sparse_desc = bell_draw(streams_of[3], (M // S_SUB, S_SUB, DESC), 1.0, 6.0, ((0, 16), (1, 32)))
    panel_block = jax.random.randint(streams_of[4], (), 0, M // PANEL).astype(jnp.int32)
    return {"env_desc": env_desc, "env_counts": env_counts, "reg_desc": reg_desc, "sparse_desc": sparse_desc, "panel_block": panel_block}


cube_scale = 15.0 ** (-0.5)

def kernel(left_desc, right_desc):
    scaled = lax.dot_general(left_desc.astype(jnp.float32), right_desc.astype(jnp.float32), (((1,), (1,)), ((), ())), preferred_element_type=jnp.float32) * DESC ** (-0.5)
    return scaled * scaled * scaled * cube_scale

def energy_rows(counts, kernel_rows):
    finish = jnp.cumsum(counts).astype(jnp.int32)
    starts = (finish - counts).astype(jnp.int32)
    position = jnp.arange(kernel_rows.shape[0], dtype=jnp.int32)[None, :]
    member = (position >= starts[:, None]) & (position < finish[:, None])
    weights = member.astype(jnp.float32) / counts.astype(jnp.float32)[:, None]
    return jnp.dot(weights, kernel_rows, precision=lax.Precision.HIGHEST)

def reference(env_desc, env_counts, reg_desc, sparse_desc, panel_block):
    points = sparse_desc.reshape(M, DESC)

    def block_rows(pieces):
        descriptors, counts, reg_rows = pieces
        kernel_rows = kernel(descriptors, points)
        return jnp.concatenate([energy_rows(counts, kernel_rows), kernel(reg_rows, points)], 0)
    design = lax.map(block_rows, (env_desc.reshape(N_ENV, ENV_DEV, DESC), env_counts, reg_desc.reshape(N_ENV, REG_DEV, DESC)))
    design = design.reshape(ROWS, M)
    offset = (panel_block * PANEL).astype(jnp.int32)
    panel_cols = lax.dynamic_slice_in_dim(design, offset, PANEL, 1)
    orthogonal, upper = jnp.linalg.qr(panel_cols)
    diag_signs = jnp.sign(jnp.diagonal(upper))
    orthogonal = orthogonal * diag_signs[None, :]
    coupling = lax.dot_general(orthogonal, design, (((0,), (0,)), ((), ())), precision=lax.Precision.HIGHEST)
    column = jnp.arange(M, dtype=jnp.int32)
    coupling = jnp.where(column[None, :] >= offset, coupling, jnp.zeros_like(coupling))
    updated = design - jnp.dot(orthogonal, coupling, precision=lax.Precision.HIGHEST)
    updated = lax.dynamic_update_slice_in_dim(updated, orthogonal, offset, 1)
    return (updated, coupling)
```

```python
import jax
import jax.numpy as jnp
from jax import lax
from jax.experimental import pallas as pl
from jax.experimental.pallas import tpu as pltpu
from jax.sharding import PartitionSpec as P

DESC = 1000
PANEL = 256
TILE = 256
N_Z = 16
N_SP = 16
CONF = 448
ENV = 1024
REG = 64
ROWS = CONF + REG
SLOTS = 5
COLS = SLOTS * PANEL
HALF = PANEL // 2
START = 0.95

cube_scale = 15.0 ** (-0.5)
dot_scale = DESC ** (-0.5)
VMEM_LIMIT = 60 * 1024 * 1024

SAME_CORE = [[2 * z + c for z in range(N_Z)] for c in range(2)]
CORE_SWAP = [(i, i ^ 1) for i in range(2 * N_Z)]


def nt(a, b):
    return lax.dot_general(a, b, (((1,), (1,)), ((), ())), preferred_element_type=jnp.float32)


def nn(a, b):
    return lax.dot_general(a, b, (((1,), (0,)), ((), ())), preferred_element_type=jnp.float32)


def halves(x):
    hi = x.astype(jnp.bfloat16)
    lo = (x - hi.astype(jnp.float32)).astype(jnp.bfloat16)
    return hi, lo


def cubed(product):
    scaled = product * dot_scale
    return scaled * scaled * scaled * cube_scale


def panel_kernel(points, env, reg, starts, finish, inverse, panel_ref, hi_ref, lo_ref, gram_ref, member_ref):
    position = lax.broadcasted_iota(jnp.int32, (CONF, ENV), 1)
    inside = (position >= starts[...]) & (position < finish[...])
    member = inside.astype(jnp.float32).astype(jnp.bfloat16)
    member_ref[...] = member
    pts = points[...]
    hi, lo = halves(cubed(nt(pts, env[...])))
    energy = (nt(hi, member) + nt(lo, member)) * inverse[...]
    panel_t = jnp.concatenate([energy, cubed(nt(pts, reg[...]))], 1)
    panel_ref[...] = panel_t.T
    hi, lo = halves(panel_t)
    hi_ref[...] = hi
    lo_ref[...] = lo
    gram_ref[...] = lax.dot_general(
        panel_t,
        panel_t,
        (((1,), (1,)), ((), ())),
        precision=lax.Precision.HIGHEST,
        preferred_element_type=jnp.float32,
    )


def panel_step(points, env, reg, starts, finish, inverse):
    return pl.pallas_call(
        panel_kernel,
        out_shape=(
            jax.ShapeDtypeStruct((ROWS, PANEL), jnp.float32),
            jax.ShapeDtypeStruct((PANEL, ROWS), jnp.bfloat16),
            jax.ShapeDtypeStruct((PANEL, ROWS), jnp.bfloat16),
            jax.ShapeDtypeStruct((PANEL, PANEL), jnp.float32),
            jax.ShapeDtypeStruct((CONF, ENV), jnp.bfloat16),
        ),
        compiler_params=pltpu.CompilerParams(vmem_limit_bytes=VMEM_LIMIT),
        name="panel",
    )(points, env, reg, starts, finish, inverse)


def design_kernel(core, points, env, reg, member, inverse, panel_hi, panel_lo, design_ref, keep_ref, send_ref):
    pts = points[...]
    hi, lo = halves(cubed(nt(env[...], pts)))
    weights = member[...]
    energy = (nn(weights, hi) + nn(weights, lo)) * inverse[...]
    rows = jnp.concatenate([energy, cubed(nt(reg[...], pts))], 0)
    design_ref[...] = rows
    hi, lo = halves(rows)
    left = panel_hi[...]
    product = nn(left, hi) + nn(left, lo) + nn(panel_lo[...], hi)

    @pl.when(core[0] == 0)
    def _():
        keep_ref[...] = product[:HALF]
        send_ref[...] = product[HALF:]

    @pl.when(core[0] != 0)
    def _():
        keep_ref[...] = product[HALF:]
        send_ref[...] = product[:HALF]


def design_step(core, points, env, reg, member, inverse, panel_hi, panel_lo):
    vmem = pl.BlockSpec(memory_space=pltpu.VMEM)
    return pl.pallas_call(
        design_kernel,
        in_specs=[pl.BlockSpec(memory_space=pltpu.SMEM)] + [vmem] * 7,
        out_specs=(vmem, vmem, vmem),
        out_shape=(
            jax.ShapeDtypeStruct((ROWS, COLS), jnp.float32),
            jax.ShapeDtypeStruct((HALF, COLS), jnp.float32),
            jax.ShapeDtypeStruct((HALF, COLS), jnp.float32),
        ),
        compiler_params=pltpu.CompilerParams(vmem_limit_bytes=VMEM_LIMIT),
        cost_estimate=pl.CostEstimate(flops=7 * 10**9, bytes_accessed=9 * 10**6, transcendentals=0),
        name="design",
    )(core, points, env, reg, member, inverse, panel_hi, panel_lo)


FULL = dict(precision=lax.Precision.HIGHEST, preferred_element_type=jnp.float32)


def stacked(core, own, other):
    return jnp.where(core == 0, jnp.concatenate([own, other], 0), jnp.concatenate([other, own], 0))


def factor_kernel(core, own, other, inv_ref, x_ref, s_ref):
    row = lax.broadcasted_iota(jnp.int32, (PANEL, PANEL), 0)
    col = lax.broadcasted_iota(jnp.int32, (PANEL, PANEL), 1)
    diag = (row == col).astype(jnp.float32)
    phi = jnp.where(row > col, 1.0, 0.5 * diag)
    g = stacked(core[0], own[...], other[...])
    on_diag = g * diag
    d_row = lax.rsqrt(jnp.sum(on_diag, 0, keepdims=True))
    d_col = lax.rsqrt(jnp.sum(on_diag, 1, keepdims=True))
    scaled = g * d_row * d_col
    x = START * (diag - phi * (START * START * scaled - diag))
    low = scaled.astype(jnp.bfloat16)
    for _ in range(2):
        x_low = x.astype(jnp.bfloat16)
        error = nt(nn(x_low, low).astype(jnp.bfloat16), x_low) - diag
        x = x - nn((phi * error).astype(jnp.bfloat16), x_low)
    x_ref[...] = x
    s_ref[...] = scaled

    def more(state):
        step, size = state
        return (step < 12) & (size >= 1e-6) & (size < 1e6)

    def refine(state):
        x = x_ref[...]
        half = lax.dot_general(x, s_ref[...], (((1,), (0,)), ((), ())), **FULL)
        error = lax.dot_general(half, x, (((1,), (1,)), ((), ())), **FULL) - diag
        x_ref[...] = x - nn((phi * error).astype(jnp.bfloat16), x.astype(jnp.bfloat16))
        return state[0] + 1, jnp.sum(error * error)

    _, size = lax.while_loop(more, refine, (0, jnp.float32(1.0)))
    inv_ref[...] = x_ref[...] * d_row

    @pl.when(jnp.logical_not(size < 1e-6))
    def _():
        x_ref[...] = diag
        s_ref[...] = scaled
        index = lax.broadcasted_iota(jnp.int32, (PANEL, 1), 0)
        lane = lax.broadcasted_iota(jnp.int32, (1, PANEL), 1)

        def eliminate(j, carry):
            s = s_ref[...]
            s_row = s_ref[pl.ds(j, 1), :]
            x_row = x_ref[pl.ds(j, 1), :]
            pivot = jnp.sum(jnp.where(lane == j, s_row, 0.0), 1, keepdims=True)
            column = jnp.sum(jnp.where(lane == j, s, 0.0), 1, keepdims=True)
            below = jnp.where(index > j, column / pivot, 0.0)
            s_ref[...] = s - below * s_row
            x = x_ref[...] - below * x_row
            x_ref[...] = jnp.where(index == j, x * lax.rsqrt(pivot), x)
            return carry

        lax.fori_loop(0, PANEL, eliminate, 0)
        inv_ref[...] = x_ref[...] * d_row


def factor_step(core, own, other):
    vmem = pl.BlockSpec(memory_space=pltpu.VMEM)
    return pl.pallas_call(
        factor_kernel,
        in_specs=[pl.BlockSpec(memory_space=pltpu.SMEM), vmem, vmem],
        out_specs=vmem,
        out_shape=jax.ShapeDtypeStruct((PANEL, PANEL), jnp.float32),
        scratch_shapes=[pltpu.VMEM((PANEL, PANEL), jnp.float32)] * 2,
        compiler_params=pltpu.CompilerParams(vmem_limit_bytes=VMEM_LIMIT),
        name="factor",
    )(core, own, other)


def update_kernel(slot, design, own, other, inverse_factor, panel, updated_ref, coupling_ref, q_ref):
    t = pl.program_id(0)

    @pl.when(t == 0)
    def _():
        p_hi, p_lo = halves(panel[...])
        f_hi, f_lo = halves(inverse_factor[...])
        q_ref[...] = nt(p_hi, f_hi) + nt(p_hi, f_lo) + nt(p_lo, f_hi)

    @pl.when(t < slot[0])
    def _():
        updated_ref[...] = design[...]
        coupling_ref[...] = jnp.zeros((PANEL, TILE), jnp.float32)

    @pl.when(t >= slot[0])
    def _():
        f_hi, f_lo = halves(inverse_factor[...])
        w_hi, w_lo = halves(stacked(slot[1], own[...], other[...]))
        coupling = nn(f_hi, w_hi) + nn(f_hi, w_lo) + nn(f_lo, w_hi)
        coupling_ref[...] = coupling
        q_hi, q_lo = halves(q_ref[...])
        c_hi, c_lo = halves(coupling)
        updated_ref[...] = design[...] - (nn(q_hi, c_hi) + nn(q_hi, c_lo) + nn(q_lo, c_hi))

    @pl.when(t == slot[0])
    def _():
        updated_ref[...] = q_ref[...]


def update_step(slot, design, own, other, inverse_factor, panel):
    return pl.pallas_call(
        update_kernel,
        grid_spec=pltpu.PrefetchScalarGridSpec(
            num_scalar_prefetch=1,
            grid=(SLOTS,),
            in_specs=[
                pl.BlockSpec((ROWS, TILE), lambda t, s: (0, t)),
                pl.BlockSpec((HALF, TILE), lambda t, s: (0, t)),
                pl.BlockSpec((HALF, TILE), lambda t, s: (0, t)),
                pl.BlockSpec((PANEL, PANEL), lambda t, s: (0, 0)),
                pl.BlockSpec((ROWS, PANEL), lambda t, s: (0, 0)),
            ],
            out_specs=(
                pl.BlockSpec((ROWS, TILE), lambda t, s: (0, t)),
                pl.BlockSpec((PANEL, TILE), lambda t, s: (0, t)),
            ),
            scratch_shapes=[pltpu.VMEM((ROWS, PANEL), jnp.float32)],
        ),
        out_shape=(
            jax.ShapeDtypeStruct((ROWS, COLS), jnp.float32),
            jax.ShapeDtypeStruct((PANEL, COLS), jnp.float32),
        ),
        compiler_params=pltpu.CompilerParams(vmem_limit_bytes=VMEM_LIMIT),
        name="update",
    )(slot, design, own, other, inverse_factor, panel)


def shards(env_desc, env_counts, reg_desc, sparse_desc, panel_block):
    core = lax.axis_index("env") % 2
    column_shard = lax.axis_index("sp")
    owner = panel_block // SLOTS

    gathered = lax.all_gather(sparse_desc, "env", axis=1, tiled=True)

    with jax.named_scope("panel_points"):
        mine = lax.dynamic_index_in_dim(sparse_desc, panel_block - owner * SLOTS, 0, keepdims=False)
        offered = jnp.broadcast_to(mine[None], (N_SP,) + mine.shape)
        offered = lax.all_to_all(offered, "sp", 0, 0)
        mine = lax.dynamic_index_in_dim(offered, owner, 0, keepdims=False)
        panel_points = lax.all_gather(mine, "env", axis=0, tiled=True)

    counts = env_counts[0]
    finish = jnp.cumsum(counts)
    starts = finish - counts
    inverse = 1.0 / counts.astype(jnp.float32)
    panel, panel_hi, panel_lo, gram, member = panel_step(
        panel_points, env_desc, reg_desc, starts[:, None], finish[:, None], inverse[None, :]
    )

    with jax.named_scope("gram"):
        pieces = gram.reshape(2, N_Z, HALF // N_Z, PANEL).swapaxes(0, 1)
        pieces = pieces.reshape(2 * N_Z, HALF // N_Z, PANEL)
        gram_rows = jnp.sum(lax.all_to_all(pieces, "env", 0, 0), 0)

    core_index = core.reshape(1).astype(jnp.int32)
    points = gathered.reshape(COLS, DESC)
    design, keep, send = design_step(
        core_index, points, env_desc, reg_desc, member, inverse[:, None], panel_hi, panel_lo
    )

    with jax.named_scope("product"):
        send, gram_rows = lax.optimization_barrier((send, gram_rows))
        keep = keep + lax.ppermute(send, "env", CORE_SWAP)
        keep = keep.reshape(N_Z, HALF // N_Z, COLS)
        keep = lax.all_to_all(keep, "env", 0, 0, axis_index_groups=SAME_CORE)
        rows = jnp.concatenate([jnp.sum(keep, 0), gram_rows], 1)
        own = lax.all_gather(rows, "env", axis=0, tiled=True, axis_index_groups=SAME_CORE)
        own_gram, own = own[:, COLS:], own[:, :COLS]
        other_gram = lax.ppermute(own_gram, "env", CORE_SWAP)
        other = lax.ppermute(own, "env", CORE_SWAP)

    inverse_factor = factor_step(core_index, own_gram, other_gram)
    slot = jnp.stack([panel_block - column_shard * SLOTS, core]).astype(jnp.int32)
    return update_step(slot, design, own, other, inverse_factor, panel)


def solution(mesh):
    in_specs = (P("env", None), P("env", None), P("env", None), P("sp", "env", None), P())
    out_specs = (P("env", "sp"), P(None, "sp"))
    return jax.shard_map(shards, mesh=mesh, in_specs=in_specs, out_specs=out_specs, check_vma=False)
```

```python
import jax
import jax.numpy as jnp
from jax import lax
from jax.experimental import pallas as pl
from jax.experimental.pallas import tpu as pltpu
from jax.sharding import PartitionSpec as P

DESC = 1000
PANEL = 256
TILE = 256
N_Z = 16
N_SP = 16
CONF = 448
ENV = 1024
REG = 64
ROWS = CONF + REG
SLOTS = 5
COLS = SLOTS * PANEL
HALF = PANEL // 2
START = 0.95

cube_scale = 15.0 ** (-0.5)
dot_scale = DESC ** (-0.5)
VMEM_LIMIT = 40 * 1024 * 1024
DESIGN_VMEM = 60 * 1024 * 1024

SAME_CORE = [[2 * z + c for z in range(N_Z)] for c in range(2)]
CORE_SWAP = [(i, i ^ 1) for i in range(2 * N_Z)]


def nt(a, b):
    return lax.dot_general(a, b, (((1,), (1,)), ((), ())), preferred_element_type=jnp.float32)


def nn(a, b):
    return lax.dot_general(a, b, (((1,), (0,)), ((), ())), preferred_element_type=jnp.float32)


def halves(x):
    hi = x.astype(jnp.bfloat16)
    lo = (x - hi.astype(jnp.float32)).astype(jnp.bfloat16)
    return hi, lo


def cubed(product):
    scaled = product * dot_scale
    return scaled * scaled * scaled * cube_scale


def panel_kernel(points, env, reg, starts, finish, inverse, panel_ref, hi_ref, lo_ref, gram_ref, member_ref):
    position = lax.broadcasted_iota(jnp.int32, (CONF, ENV), 1)
    inside = (position >= starts[...]) & (position < finish[...])
    member = inside.astype(jnp.float32).astype(jnp.bfloat16)
    member_ref[...] = member
    pts = points[...]
    hi, lo = halves(cubed(nt(pts, env[...])))
    energy = (nt(hi, member) + nt(lo, member)) * inverse[...]
    panel_t = jnp.concatenate([energy, cubed(nt(pts, reg[...]))], 1)
    panel_ref[...] = panel_t.T
    hi, lo = halves(panel_t)
    hi_ref[...] = hi
    lo_ref[...] = lo
    gram_ref[...] = lax.dot_general(
        panel_t,
        panel_t,
        (((1,), (1,)), ((), ())),
        precision=lax.Precision.HIGHEST,
        preferred_element_type=jnp.float32,
    )


def panel_step(points, env, reg, starts, finish, inverse):
    return pl.pallas_call(
        panel_kernel,
        out_shape=(
            jax.ShapeDtypeStruct((ROWS, PANEL), jnp.float32),
            jax.ShapeDtypeStruct((PANEL, ROWS), jnp.bfloat16),
            jax.ShapeDtypeStruct((PANEL, ROWS), jnp.bfloat16),
            jax.ShapeDtypeStruct((PANEL, PANEL), jnp.float32),
            jax.ShapeDtypeStruct((CONF, ENV), jnp.bfloat16),
        ),
        compiler_params=pltpu.CompilerParams(vmem_limit_bytes=VMEM_LIMIT),
        name="panel",
    )(points, env, reg, starts, finish, inverse)


def design_kernel(
    place, points, env, reg, member, inverse, panel_hi, panel_lo, design_ref, keep_ref, send_ref, rows_ref, sem
):
    pts = points[...]
    hi, lo = halves(cubed(nt(env[...], pts)))
    weights = member[...]
    rows_ref[:CONF] = (nn(weights, hi) + nn(weights, lo)) * inverse[...]
    rows_ref[CONF:] = cubed(nt(reg[...], pts))
    leave = pltpu.make_async_copy(rows_ref, design_ref, sem)
    leave.start()
    hi, lo = halves(rows_ref[...])
    left = panel_hi[...]
    product = nn(left, hi) + nn(left, lo) + nn(panel_lo[...], hi)
    first = place[0] == 0
    keep_ref[...] = jnp.where(first, product[:HALF], product[HALF:])
    send_ref[...] = jnp.where(first, product[HALF:], product[:HALF])
    leave.wait()


def design_step(place, points, env, reg, member, inverse, panel_hi, panel_lo):
    half = pl.BlockSpec((HALF, COLS), lambda t, s: (0, 0))
    arrays = (points, env, reg, member, inverse, panel_hi, panel_lo)
    return pl.pallas_call(
        design_kernel,
        grid_spec=pltpu.PrefetchScalarGridSpec(
            num_scalar_prefetch=1,
            grid=(1,),
            in_specs=[pl.BlockSpec(a.shape, lambda t, s: (0, 0)) for a in arrays],
            out_specs=(pl.BlockSpec(memory_space=pl.ANY), half, half),
            scratch_shapes=[pltpu.VMEM((ROWS, COLS), jnp.float32), pltpu.SemaphoreType.DMA],
        ),
        out_shape=(
            jax.ShapeDtypeStruct((ROWS, COLS), jnp.float32),
            jax.ShapeDtypeStruct((HALF, COLS), jnp.float32),
            jax.ShapeDtypeStruct((HALF, COLS), jnp.float32),
        ),
        compiler_params=pltpu.CompilerParams(vmem_limit_bytes=DESIGN_VMEM),
        cost_estimate=pl.CostEstimate(flops=7 * 10**9, bytes_accessed=9 * 10**6, transcendentals=0),
        name="design",
    )(place, *arrays)


FULL = dict(precision=lax.Precision.HIGHEST, preferred_element_type=jnp.float32)


def stacked(core, own, other):
    return jnp.where(core == 0, jnp.concatenate([own, other], 0), jnp.concatenate([other, own], 0))


def factor_kernel(core, own, other, inv_ref, x_ref, s_ref):
    row = lax.broadcasted_iota(jnp.int32, (PANEL, PANEL), 0)
    col = lax.broadcasted_iota(jnp.int32, (PANEL, PANEL), 1)
    diag = (row == col).astype(jnp.float32)
    phi = jnp.where(row > col, 1.0, 0.5 * diag)
    g = stacked(core[0], own[...], other[...])
    on_diag = g * diag
    d_row = lax.rsqrt(jnp.sum(on_diag, 0, keepdims=True))
    d_col = lax.rsqrt(jnp.sum(on_diag, 1, keepdims=True))
    scaled = g * d_row * d_col
    x = START * (diag - phi * (START * START * scaled - diag))
    low = scaled.astype(jnp.bfloat16)
    for _ in range(2):
        x_low = x.astype(jnp.bfloat16)
        error = nt(nn(x_low, low).astype(jnp.bfloat16), x_low) - diag
        x = x - nn((phi * error).astype(jnp.bfloat16), x_low)
    x_ref[...] = x
    s_ref[...] = scaled

    def more(state):
        step, size = state
        return (step < 12) & (size >= 1e-6) & (size < 1e6)

    def refine(state):
        x = x_ref[...]
        half = lax.dot_general(x, s_ref[...], (((1,), (0,)), ((), ())), **FULL)
        error = lax.dot_general(half, x, (((1,), (1,)), ((), ())), **FULL) - diag
        x_ref[...] = x - nn((phi * error).astype(jnp.bfloat16), x.astype(jnp.bfloat16))
        return state[0] + 1, jnp.sum(error * error)

    _, size = lax.while_loop(more, refine, (0, jnp.float32(1.0)))
    inv_ref[...] = x_ref[...] * d_row

    @pl.when(jnp.logical_not(size < 1e-6))
    def _():
        x_ref[...] = diag
        s_ref[...] = scaled
        index = lax.broadcasted_iota(jnp.int32, (PANEL, 1), 0)
        lane = lax.broadcasted_iota(jnp.int32, (1, PANEL), 1)

        def eliminate(j, carry):
            s = s_ref[...]
            s_row = s_ref[pl.ds(j, 1), :]
            x_row = x_ref[pl.ds(j, 1), :]
            pivot = jnp.sum(jnp.where(lane == j, s_row, 0.0), 1, keepdims=True)
            column = jnp.sum(jnp.where(lane == j, s, 0.0), 1, keepdims=True)
            below = jnp.where(index > j, column / pivot, 0.0)
            s_ref[...] = s - below * s_row
            x = x_ref[...] - below * x_row
            x_ref[...] = jnp.where(index == j, x * lax.rsqrt(pivot), x)
            return carry

        lax.fori_loop(0, PANEL, eliminate, 0)
        inv_ref[...] = x_ref[...] * d_row


def factor_step(place, own, other):
    columns = pl.BlockSpec((HALF, PANEL), lambda t, s: (0, SLOTS))
    return pl.pallas_call(
        factor_kernel,
        grid_spec=pltpu.PrefetchScalarGridSpec(
            num_scalar_prefetch=1,
            grid=(1,),
            in_specs=[columns, columns],
            out_specs=pl.BlockSpec((PANEL, PANEL), lambda t, s: (0, 0)),
            scratch_shapes=[pltpu.VMEM((PANEL, PANEL), jnp.float32)] * 2,
        ),
        out_shape=jax.ShapeDtypeStruct((PANEL, PANEL), jnp.float32),
        compiler_params=pltpu.CompilerParams(vmem_limit_bytes=VMEM_LIMIT),
        name="factor",
    )(place, own, other)


def update_kernel(place, design, own, other, inverse_factor, panel, updated_ref, coupling_ref, q_ref):
    t = pl.program_id(0)

    @pl.when(t == 0)
    def _():
        p_hi, p_lo = halves(panel[...])
        f_hi, f_lo = halves(inverse_factor[...])
        q_ref[...] = nt(p_hi, f_hi) + nt(p_hi, f_lo) + nt(p_lo, f_hi)

    @pl.when(t < place[1])
    def _():
        updated_ref[...] = design[...]
        coupling_ref[...] = jnp.zeros((PANEL, TILE), jnp.float32)

    @pl.when(t >= place[1])
    def _():
        f_hi, f_lo = halves(inverse_factor[...])
        w_hi, w_lo = halves(stacked(place[0], own[...], other[...]))
        coupling = nn(f_hi, w_hi) + nn(f_hi, w_lo) + nn(f_lo, w_hi)
        coupling_ref[...] = coupling
        q_hi, q_lo = halves(q_ref[...])
        c_hi, c_lo = halves(coupling)
        updated_ref[...] = design[...] - (nn(q_hi, c_hi) + nn(q_hi, c_lo) + nn(q_lo, c_hi))

    @pl.when(t == place[1])
    def _():
        updated_ref[...] = q_ref[...]


def update_step(place, design, own, other, inverse_factor, panel):
    return pl.pallas_call(
        update_kernel,
        grid_spec=pltpu.PrefetchScalarGridSpec(
            num_scalar_prefetch=1,
            grid=(SLOTS,),
            in_specs=[
                pl.BlockSpec((ROWS, TILE), lambda t, s: (0, t)),
                pl.BlockSpec((HALF, TILE), lambda t, s: (0, t)),
                pl.BlockSpec((HALF, TILE), lambda t, s: (0, t)),
                pl.BlockSpec((PANEL, PANEL), lambda t, s: (0, 0)),
                pl.BlockSpec((ROWS, PANEL), lambda t, s: (0, 0)),
            ],
            out_specs=(
                pl.BlockSpec((ROWS, TILE), lambda t, s: (0, t)),
                pl.BlockSpec((PANEL, TILE), lambda t, s: (0, t)),
            ),
            scratch_shapes=[pltpu.VMEM((ROWS, PANEL), jnp.float32)],
        ),
        out_shape=(
            jax.ShapeDtypeStruct((ROWS, COLS), jnp.float32),
            jax.ShapeDtypeStruct((PANEL, COLS), jnp.float32),
        ),
        compiler_params=pltpu.CompilerParams(vmem_limit_bytes=VMEM_LIMIT),
        name="update",
    )(place, design, own, other, inverse_factor, panel)


def shards(env_desc, env_counts, reg_desc, sparse_desc, panel_block):
    core = lax.axis_index("env") % 2
    column_shard = lax.axis_index("sp")
    owner = panel_block // SLOTS

    gathered = lax.all_gather(sparse_desc, "env", axis=1, tiled=True)

    with jax.named_scope("panel_points"):
        mine = lax.dynamic_index_in_dim(sparse_desc, panel_block - owner * SLOTS, 0, keepdims=False)
        offered = jnp.broadcast_to(mine[None], (N_SP,) + mine.shape)
        offered = lax.all_to_all(offered, "sp", 0, 0)
        mine = lax.dynamic_index_in_dim(offered, owner, 0, keepdims=False)
        panel_points = lax.all_gather(mine, "env", axis=0, tiled=True)

    counts = env_counts[0]
    finish = jnp.cumsum(counts)
    starts = finish - counts
    inverse = 1.0 / counts.astype(jnp.float32)
    place = jnp.stack([core, panel_block - column_shard * SLOTS]).astype(jnp.int32)
    panel, panel_hi, panel_lo, gram, member = panel_step(
        panel_points, env_desc, reg_desc, starts[:, None], finish[:, None], inverse[None, :]
    )

    with jax.named_scope("gram"):
        pieces = gram.reshape(2, N_Z, HALF // N_Z, PANEL).swapaxes(0, 1)
        pieces = pieces.reshape(2 * N_Z, HALF // N_Z, PANEL)
        pieces = lax.all_to_all(pieces, "env", 0, 0)

    points = gathered.reshape(COLS, DESC)
    design, keep, send = design_step(
        place, points, env_desc, reg_desc, member, inverse[:, None], panel_hi, panel_lo
    )

    with jax.named_scope("product"):
        send, pieces = lax.optimization_barrier((send, pieces))
        keep = keep + lax.ppermute(send, "env", CORE_SWAP)
        keep = keep.reshape(N_Z, HALF // N_Z, COLS)
        keep = lax.all_to_all(keep, "env", 0, 0, axis_index_groups=SAME_CORE)
        rows = jnp.concatenate([jnp.sum(keep, 0), jnp.sum(pieces, 0)], 1)
        own = lax.all_gather(rows, "env", axis=0, tiled=True, axis_index_groups=SAME_CORE)
        other = lax.ppermute(own, "env", CORE_SWAP)

    inverse_factor = factor_step(place, own, other)
    return update_step(place, design, own, other, inverse_factor, panel)


def solution(mesh):
    in_specs = (P("env", None), P("env", None), P("env", None), P("sp", "env", None), P())
    out_specs = (P("env", "sp"), P(None, "sp"))
    return jax.shard_map(shards, mesh=mesh, in_specs=in_specs, out_specs=out_specs, check_vma=False)
```

```python
import jax
import jax.numpy as jnp
from jax import lax
from jax.experimental import pallas as pl
from jax.experimental.pallas import tpu as pltpu
from jax.sharding import PartitionSpec as P

DESC = 1000
PANEL = 256
TILE = 256
N_Z = 16
N_SP = 16
CONF = 448
ENV = 1024
REG = 64
ROWS = CONF + REG
SLOTS = 5
COLS = SLOTS * PANEL
HALF = PANEL // 2
START = 0.95
LANES = 128
TILES = COLS // LANES
LOW = 3
CODE = (TILES + LOW) * LANES
FIXED = 524286.0

cube_scale = 15.0 ** (-0.5)
dot_scale = DESC ** (-0.5)
VMEM_LIMIT = 40 * 1024 * 1024
DESIGN_VMEM = 60 * 1024 * 1024

SAME_CORE = [[2 * z + c for z in range(N_Z)] for c in range(2)]
CORE_SWAP = [(i, i ^ 1) for i in range(2 * N_Z)]


def nt(a, b):
    return lax.dot_general(a, b, (((1,), (1,)), ((), ())), preferred_element_type=jnp.float32)


def nn(a, b):
    return lax.dot_general(a, b, (((1,), (0,)), ((), ())), preferred_element_type=jnp.float32)


def halves(x):
    hi = x.astype(jnp.bfloat16)
    lo = (x - hi.astype(jnp.float32)).astype(jnp.bfloat16)
    return hi, lo


def cubed(product):
    scaled = product * dot_scale
    return scaled * scaled * scaled * cube_scale


def panel_kernel(points, env, reg, starts, finish, inverse, panel_ref, hi_ref, lo_ref, gram_ref, member_ref):
    position = lax.broadcasted_iota(jnp.int32, (CONF, ENV), 1)
    inside = (position >= starts[...]) & (position < finish[...])
    member = inside.astype(jnp.float32).astype(jnp.bfloat16)
    member_ref[...] = member
    pts = points[...]
    hi, lo = halves(cubed(nt(pts, env[...])))
    energy = (nt(hi, member) + nt(lo, member)) * inverse[...]
    panel_t = jnp.concatenate([energy, cubed(nt(pts, reg[...]))], 1)
    panel_ref[...] = panel_t.T
    hi, lo = halves(panel_t)
    hi_ref[...] = hi
    lo_ref[...] = lo
    gram_ref[...] = lax.dot_general(
        panel_t,
        panel_t,
        (((1,), (1,)), ((), ())),
        precision=lax.Precision.HIGHEST,
        preferred_element_type=jnp.float32,
    )


def panel_step(points, env, reg, starts, finish, inverse):
    return pl.pallas_call(
        panel_kernel,
        out_shape=(
            jax.ShapeDtypeStruct((ROWS, PANEL), jnp.float32),
            jax.ShapeDtypeStruct((PANEL, ROWS), jnp.bfloat16),
            jax.ShapeDtypeStruct((PANEL, ROWS), jnp.bfloat16),
            jax.ShapeDtypeStruct((PANEL, PANEL), jnp.float32),
            jax.ShapeDtypeStruct((CONF, ENV), jnp.bfloat16),
        ),
        compiler_params=pltpu.CompilerParams(vmem_limit_bytes=VMEM_LIMIT),
        name="panel",
    )(points, env, reg, starts, finish, inverse)


def design_kernel(
    place, points, env, reg, member, inverse, panel_hi, panel_lo, design_ref, keep_ref, send_ref, rows_ref, sem
):
    pts = points[...]
    hi, lo = halves(cubed(nt(env[...], pts)))
    weights = member[...]
    rows_ref[:CONF] = (nn(weights, hi) + nn(weights, lo)) * inverse[...]
    rows_ref[CONF:] = cubed(nt(reg[...], pts))
    leave = pltpu.make_async_copy(rows_ref, design_ref, sem)
    leave.start()
    hi, lo = halves(rows_ref[...])
    left = panel_hi[...]
    product = nn(left, hi) + nn(left, lo) + nn(panel_lo[...], hi)
    first = place[0] == 0
    keep_ref[...] = jnp.where(first, product[:HALF], product[HALF:])
    send_ref[...] = jnp.where(first, product[HALF:], product[:HALF])
    leave.wait()


def design_step(place, points, env, reg, member, inverse, panel_hi, panel_lo):
    half = pl.BlockSpec((HALF, COLS), lambda t, s: (0, 0))
    arrays = (points, env, reg, member, inverse, panel_hi, panel_lo)
    return pl.pallas_call(
        design_kernel,
        grid_spec=pltpu.PrefetchScalarGridSpec(
            num_scalar_prefetch=1,
            grid=(1,),
            in_specs=[pl.BlockSpec(a.shape, lambda t, s: (0, 0)) for a in arrays],
            out_specs=(pl.BlockSpec(memory_space=pl.ANY), half, half),
            scratch_shapes=[pltpu.VMEM((ROWS, COLS), jnp.float32), pltpu.SemaphoreType.DMA],
        ),
        out_shape=(
            jax.ShapeDtypeStruct((ROWS, COLS), jnp.float32),
            jax.ShapeDtypeStruct((HALF, COLS), jnp.float32),
            jax.ShapeDtypeStruct((HALF, COLS), jnp.float32),
        ),
        compiler_params=pltpu.CompilerParams(vmem_limit_bytes=DESIGN_VMEM),
        cost_estimate=pl.CostEstimate(flops=7 * 10**9, bytes_accessed=9 * 10**6, transcendentals=0),
        name="design",
    )(place, *arrays)


def tile_of(t):
    return slice(t * LANES, (t + 1) * LANES)


def code_kernel(keep, received, code_ref):
    lane = lax.broadcasted_iota(jnp.int32, (HALF, LANES), 1)
    low = [jnp.zeros((HALF, LANES), jnp.int32) for _ in range(LOW)]
    for t in range(TILES):
        x = keep[:, tile_of(t)] + received[:, tile_of(t)]
        largest = jnp.maximum(jnp.max(jnp.abs(x), 1, keepdims=True), 1e-30)
        exponent = jnp.minimum(jnp.ceil(jnp.log2(largest) + 1e-4), 127.0)
        scaled = jnp.clip(x * (jnp.exp2(-exponent) * FIXED), -FIXED, FIXED)
        rounded = jnp.where(scaled < 0, scaled - 0.5, scaled + 0.5).astype(jnp.int32)
        code_ref[:, tile_of(t)] = (rounded >> 4).astype(jnp.int16)
        low[t // 4] = low[t // 4] + ((rounded & 15) << (4 * (t % 4)))
        low[-1] = low[-1] + jnp.where(lane == t, (exponent.astype(jnp.int32) + 128) << 8, 0)
    for k in range(LOW):
        code_ref[:, tile_of(TILES + k)] = (low[k] - 32768).astype(jnp.int16)


def sum_kernel(code, pieces, rows_ref):
    lane = lax.broadcasted_iota(jnp.int32, (HALF, LANES), 1)
    low = [code[:, tile_of(TILES + k)].astype(jnp.int32) + 32768 for k in range(LOW)]
    exponents = (low[-1] >> 8) - 128
    for t in range(TILES):
        exponent = jnp.sum(jnp.where(lane == t, exponents, 0).astype(jnp.float32), 1, keepdims=True)
        fixed = code[:, tile_of(t)].astype(jnp.int32) * 16 + ((low[t // 4] >> (4 * (t % 4))) & 15)
        x = fixed.astype(jnp.float32) * (jnp.exp2(exponent) * (1.0 / FIXED))
        rows_ref[:, tile_of(t)] = jnp.sum(x.reshape(N_Z, HALF // N_Z, LANES), 0)
    rows_ref[:, COLS:] = jnp.sum(pieces[...], 0)


def code_step(keep, received):
    half = pl.BlockSpec((HALF, COLS), lambda t: (0, 0))
    return pl.pallas_call(
        code_kernel,
        grid=(1,),
        in_specs=[half, half],
        out_specs=pl.BlockSpec((HALF, CODE), lambda t: (0, 0)),
        out_shape=jax.ShapeDtypeStruct((HALF, CODE), jnp.int16),
        compiler_params=pltpu.CompilerParams(vmem_limit_bytes=DESIGN_VMEM),
        name="code",
    )(keep, received)


def sum_step(code, pieces):
    vmem = pl.BlockSpec(memory_space=pltpu.VMEM)
    return pl.pallas_call(
        sum_kernel,
        in_specs=[vmem, vmem],
        out_specs=vmem,
        out_shape=jax.ShapeDtypeStruct((HALF // N_Z, COLS + PANEL), jnp.float32),
        compiler_params=pltpu.CompilerParams(vmem_limit_bytes=VMEM_LIMIT),
        name="sum",
    )(code, pieces)


FULL = dict(precision=lax.Precision.HIGHEST, preferred_element_type=jnp.float32)


def stacked(core, own, other):
    return jnp.where(core == 0, jnp.concatenate([own, other], 0), jnp.concatenate([other, own], 0))


def factor_kernel(core, own, other, inv_ref, x_ref, s_ref):
    row = lax.broadcasted_iota(jnp.int32, (PANEL, PANEL), 0)
    col = lax.broadcasted_iota(jnp.int32, (PANEL, PANEL), 1)
    diag = (row == col).astype(jnp.float32)
    phi = jnp.where(row > col, 1.0, 0.5 * diag)
    g = stacked(core[0], own[...], other[...])
    on_diag = g * diag
    d_row = lax.rsqrt(jnp.sum(on_diag, 0, keepdims=True))
    d_col = lax.rsqrt(jnp.sum(on_diag, 1, keepdims=True))
    scaled = g * d_row * d_col
    x = START * (diag - phi * (START * START * scaled - diag))
    low = scaled.astype(jnp.bfloat16)
    for _ in range(2):
        x_low = x.astype(jnp.bfloat16)
        error = nt(nn(x_low, low).astype(jnp.bfloat16), x_low) - diag
        x = x - nn((phi * error).astype(jnp.bfloat16), x_low)
    x_ref[...] = x
    s_ref[...] = scaled

    def more(state):
        step, size = state
        return (step < 12) & (size >= 1e-6) & (size < 1e6)

    def refine(state):
        x = x_ref[...]
        half = lax.dot_general(x, s_ref[...], (((1,), (0,)), ((), ())), **FULL)
        error = lax.dot_general(half, x, (((1,), (1,)), ((), ())), **FULL) - diag
        x_ref[...] = x - nn((phi * error).astype(jnp.bfloat16), x.astype(jnp.bfloat16))
        return state[0] + 1, jnp.sum(error * error)

    _, size = lax.while_loop(more, refine, (0, jnp.float32(1.0)))
    inv_ref[...] = x_ref[...] * d_row

    @pl.when(jnp.logical_not(size < 1e-6))
    def _():
        x_ref[...] = diag
        s_ref[...] = scaled
        index = lax.broadcasted_iota(jnp.int32, (PANEL, 1), 0)
        lane = lax.broadcasted_iota(jnp.int32, (1, PANEL), 1)

        def eliminate(j, carry):
            s = s_ref[...]
            s_row = s_ref[pl.ds(j, 1), :]
            x_row = x_ref[pl.ds(j, 1), :]
            pivot = jnp.sum(jnp.where(lane == j, s_row, 0.0), 1, keepdims=True)
            column = jnp.sum(jnp.where(lane == j, s, 0.0), 1, keepdims=True)
            below = jnp.where(index > j, column / pivot, 0.0)
            s_ref[...] = s - below * s_row
            x = x_ref[...] - below * x_row
            x_ref[...] = jnp.where(index == j, x * lax.rsqrt(pivot), x)
            return carry

        lax.fori_loop(0, PANEL, eliminate, 0)
        inv_ref[...] = x_ref[...] * d_row


def factor_step(place, own, other):
    columns = pl.BlockSpec((HALF, PANEL), lambda t, s: (0, SLOTS))
    return pl.pallas_call(
        factor_kernel,
        grid_spec=pltpu.PrefetchScalarGridSpec(
            num_scalar_prefetch=1,
            grid=(1,),
            in_specs=[columns, columns],
            out_specs=pl.BlockSpec((PANEL, PANEL), lambda t, s: (0, 0)),
            scratch_shapes=[pltpu.VMEM((PANEL, PANEL), jnp.float32)] * 2,
        ),
        out_shape=jax.ShapeDtypeStruct((PANEL, PANEL), jnp.float32),
        compiler_params=pltpu.CompilerParams(vmem_limit_bytes=VMEM_LIMIT),
        name="factor",
    )(place, own, other)


def update_kernel(place, design, own, other, inverse_factor, panel, updated_ref, coupling_ref, q_ref):
    t = pl.program_id(0)

    @pl.when(t == 0)
    def _():
        p_hi, p_lo = halves(panel[...])
        f_hi, f_lo = halves(inverse_factor[...])
        q_ref[...] = nt(p_hi, f_hi) + nt(p_hi, f_lo) + nt(p_lo, f_hi)

    @pl.when(t < place[1])
    def _():
        updated_ref[...] = design[...]
        coupling_ref[...] = jnp.zeros((PANEL, TILE), jnp.float32)

    @pl.when(t >= place[1])
    def _():
        f_hi, f_lo = halves(inverse_factor[...])
        w_hi, w_lo = halves(stacked(place[0], own[...], other[...]))
        coupling = nn(f_hi, w_hi) + nn(f_hi, w_lo) + nn(f_lo, w_hi)
        coupling_ref[...] = coupling
        q_hi, q_lo = halves(q_ref[...])
        c_hi, c_lo = halves(coupling)
        updated_ref[...] = design[...] - (nn(q_hi, c_hi) + nn(q_hi, c_lo) + nn(q_lo, c_hi))

    @pl.when(t == place[1])
    def _():
        updated_ref[...] = q_ref[...]


def update_step(place, design, own, other, inverse_factor, panel):
    return pl.pallas_call(
        update_kernel,
        grid_spec=pltpu.PrefetchScalarGridSpec(
            num_scalar_prefetch=1,
            grid=(SLOTS,),
            in_specs=[
                pl.BlockSpec((ROWS, TILE), lambda t, s: (0, t)),
                pl.BlockSpec((HALF, TILE), lambda t, s: (0, t)),
                pl.BlockSpec((HALF, TILE), lambda t, s: (0, t)),
                pl.BlockSpec((PANEL, PANEL), lambda t, s: (0, 0)),
                pl.BlockSpec((ROWS, PANEL), lambda t, s: (0, 0)),
            ],
            out_specs=(
                pl.BlockSpec((ROWS, TILE), lambda t, s: (0, t)),
                pl.BlockSpec((PANEL, TILE), lambda t, s: (0, t)),
            ),
            scratch_shapes=[pltpu.VMEM((ROWS, PANEL), jnp.float32)],
        ),
        out_shape=(
            jax.ShapeDtypeStruct((ROWS, COLS), jnp.float32),
            jax.ShapeDtypeStruct((PANEL, COLS), jnp.float32),
        ),
        compiler_params=pltpu.CompilerParams(vmem_limit_bytes=VMEM_LIMIT),
        name="update",
    )(place, design, own, other, inverse_factor, panel)


def shards(env_desc, env_counts, reg_desc, sparse_desc, panel_block):
    core = lax.axis_index("env") % 2
    column_shard = lax.axis_index("sp")
    owner = panel_block // SLOTS

    gathered = lax.all_gather(sparse_desc, "env", axis=1, tiled=True)

    with jax.named_scope("panel_points"):
        mine = lax.dynamic_index_in_dim(sparse_desc, panel_block - owner * SLOTS, 0, keepdims=False)
        offered = jnp.broadcast_to(mine[None], (N_SP,) + mine.shape)
        offered = lax.all_to_all(offered, "sp", 0, 0)
        mine = lax.dynamic_index_in_dim(offered, owner, 0, keepdims=False)
        panel_points = lax.all_gather(mine, "env", axis=0, tiled=True)

    counts = env_counts[0]
    finish = jnp.cumsum(counts)
    starts = finish - counts
    inverse = 1.0 / counts.astype(jnp.float32)
    place = jnp.stack([core, panel_block - column_shard * SLOTS]).astype(jnp.int32)
    panel, panel_hi, panel_lo, gram, member = panel_step(
        panel_points, env_desc, reg_desc, starts[:, None], finish[:, None], inverse[None, :]
    )

    with jax.named_scope("gram"):
        pieces = gram.reshape(2, N_Z, HALF // N_Z, PANEL).swapaxes(0, 1)
        pieces = pieces.reshape(2 * N_Z, HALF // N_Z, PANEL)
        pieces = lax.all_to_all(pieces, "env", 0, 0)

    points = gathered.reshape(COLS, DESC)
    design, keep, send = design_step(
        place, points, env_desc, reg_desc, member, inverse[:, None], panel_hi, panel_lo
    )

    with jax.named_scope("product"):
        send, pieces = lax.optimization_barrier((send, pieces))
        code = code_step(keep, lax.ppermute(send, "env", CORE_SWAP))
        code = code.reshape(N_Z, HALF // N_Z, CODE)
        code = lax.all_to_all(code, "env", 0, 0, axis_index_groups=SAME_CORE)
        rows = sum_step(code.reshape(HALF, CODE), pieces)
        own = lax.all_gather(rows, "env", axis=0, tiled=True, axis_index_groups=SAME_CORE)
        other = lax.ppermute(own, "env", CORE_SWAP)

    inverse_factor = factor_step(place, own, other)
    return update_step(place, design, own, other, inverse_factor, panel)


def solution(mesh):
    in_specs = (P("env", None), P("env", None), P("env", None), P("sp", "env", None), P())
    out_specs = (P("env", "sp"), P(None, "sp"))
    return jax.shard_map(shards, mesh=mesh, in_specs=in_specs, out_specs=out_specs, check_vma=False)
```

```python
import jax
import jax.numpy as jnp
from jax import lax
from jax.experimental import pallas as pl
from jax.experimental.pallas import tpu as pltpu
from jax.sharding import PartitionSpec as P

DESC = 1000
PANEL = 256
TILE = 256
N_Z = 16
N_SP = 16
CONF = 448
ENV = 1024
REG = 64
ROWS = CONF + REG
SLOTS = 5
COLS = SLOTS * PANEL
HALF = PANEL // 2
START = 0.95
LANES = 128
TILES = COLS // LANES
LOW = 3
CODE = (TILES + LOW) * LANES
FIXED = 524286.0
GRAM_FIXED = 8388606.0
WIDE = CODE + 3 * LANES
GRAM_LOW = TILES + LOW

cube_scale = 15.0 ** (-0.5)
dot_scale = DESC ** (-0.5)
VMEM_LIMIT = 40 * 1024 * 1024
DESIGN_VMEM = 60 * 1024 * 1024

SAME_CORE = [[2 * z + c for z in range(N_Z)] for c in range(2)]
CORE_SWAP = [(i, i ^ 1) for i in range(2 * N_Z)]


def nt(a, b):
    return lax.dot_general(a, b, (((1,), (1,)), ((), ())), preferred_element_type=jnp.float32)


def nn(a, b):
    return lax.dot_general(a, b, (((1,), (0,)), ((), ())), preferred_element_type=jnp.float32)


def halves(x):
    hi = x.astype(jnp.bfloat16)
    lo = (x - hi.astype(jnp.float32)).astype(jnp.bfloat16)
    return hi, lo


def cubed(product):
    scaled = product * dot_scale
    return scaled * scaled * scaled * cube_scale


def panel_kernel(points, env, reg, starts, finish, inverse, panel_ref, hi_ref, lo_ref, gram_ref, member_ref):
    position = lax.broadcasted_iota(jnp.int32, (CONF, ENV), 1)
    inside = (position >= starts[...]) & (position < finish[...])
    member = inside.astype(jnp.float32).astype(jnp.bfloat16)
    member_ref[...] = member
    pts = points[...]
    hi, lo = halves(cubed(nt(pts, env[...])))
    energy = (nt(hi, member) + nt(lo, member)) * inverse[...]
    panel_t = jnp.concatenate([energy, cubed(nt(pts, reg[...]))], 1)
    panel_ref[...] = panel_t.T
    hi, lo = halves(panel_t)
    hi_ref[...] = hi
    lo_ref[...] = lo
    gram_ref[...] = lax.dot_general(
        panel_t,
        panel_t,
        (((1,), (1,)), ((), ())),
        precision=lax.Precision.HIGHEST,
        preferred_element_type=jnp.float32,
    )


def panel_step(points, env, reg, starts, finish, inverse):
    return pl.pallas_call(
        panel_kernel,
        out_shape=(
            jax.ShapeDtypeStruct((ROWS, PANEL), jnp.float32),
            jax.ShapeDtypeStruct((PANEL, ROWS), jnp.bfloat16),
            jax.ShapeDtypeStruct((PANEL, ROWS), jnp.bfloat16),
            jax.ShapeDtypeStruct((PANEL, PANEL), jnp.float32),
            jax.ShapeDtypeStruct((CONF, ENV), jnp.bfloat16),
        ),
        compiler_params=pltpu.CompilerParams(vmem_limit_bytes=VMEM_LIMIT),
        name="panel",
    )(points, env, reg, starts, finish, inverse)


def design_kernel(
    place, points, env, reg, member, inverse, panel_hi, panel_lo, design_ref, keep_ref, send_ref, rows_ref, sem
):
    pts = points[...]
    hi, lo = halves(cubed(nt(env[...], pts)))
    weights = member[...]
    rows_ref[:CONF] = (nn(weights, hi) + nn(weights, lo)) * inverse[...]
    rows_ref[CONF:] = cubed(nt(reg[...], pts))
    leave = pltpu.make_async_copy(rows_ref, design_ref, sem)
    leave.start()
    hi, lo = halves(rows_ref[...])
    left = panel_hi[...]
    product = nn(left, hi) + nn(left, lo) + nn(panel_lo[...], hi)
    product = product.reshape(N_Z, 2, HALF // N_Z, COLS)
    first = place[0] == 0
    keep_ref[...] = jnp.where(first, product[:, 0], product[:, 1]).reshape(HALF, COLS)
    send_ref[...] = jnp.where(first, product[:, 1], product[:, 0]).reshape(HALF, COLS)
    leave.wait()


def design_step(place, points, env, reg, member, inverse, panel_hi, panel_lo):
    half = pl.BlockSpec((HALF, COLS), lambda t, s: (0, 0))
    arrays = (points, env, reg, member, inverse, panel_hi, panel_lo)
    return pl.pallas_call(
        design_kernel,
        grid_spec=pltpu.PrefetchScalarGridSpec(
            num_scalar_prefetch=1,
            grid=(1,),
            in_specs=[pl.BlockSpec(a.shape, lambda t, s: (0, 0)) for a in arrays],
            out_specs=(pl.BlockSpec(memory_space=pl.ANY), half, half),
            scratch_shapes=[pltpu.VMEM((ROWS, COLS), jnp.float32), pltpu.SemaphoreType.DMA],
        ),
        out_shape=(
            jax.ShapeDtypeStruct((ROWS, COLS), jnp.float32),
            jax.ShapeDtypeStruct((HALF, COLS), jnp.float32),
            jax.ShapeDtypeStruct((HALF, COLS), jnp.float32),
        ),
        compiler_params=pltpu.CompilerParams(vmem_limit_bytes=DESIGN_VMEM),
        cost_estimate=pl.CostEstimate(flops=7 * 10**9, bytes_accessed=9 * 10**6, transcendentals=0),
        name="design",
    )(place, *arrays)


def tile_of(t):
    return slice(t * LANES, (t + 1) * LANES)


def fixed_point(x, limit):
    largest = jnp.maximum(jnp.max(jnp.abs(x), 1, keepdims=True), 1e-30)
    exponent = jnp.minimum(jnp.ceil(jnp.log2(largest) + 1e-4), 127.0)
    scaled = jnp.clip(x * (jnp.exp2(-exponent) * limit), -limit, limit)
    return jnp.where(scaled < 0, scaled - 0.5, scaled + 0.5).astype(jnp.int32), exponent.astype(jnp.int32) + 128


def encode(tiles, code_ref):
    rows = code_ref.shape[0]
    lane = lax.broadcasted_iota(jnp.int32, (rows, LANES), 1)
    low = [jnp.zeros((rows, LANES), jnp.int32) for _ in range(LOW)]
    for t, x in enumerate(tiles):
        rounded, exponent = fixed_point(x, FIXED)
        code_ref[:, tile_of(t)] = (rounded >> 4).astype(jnp.int16)
        low[t // 4] = low[t // 4] + ((rounded & 15) << (4 * (t % 4)))
        low[-1] = low[-1] + jnp.where(lane == t, exponent << 8, 0)
    return low, lane


def unsigned(code):
    return code.astype(jnp.int32) + 32768


def unit(exponents, t, limit):
    lane = lax.broadcasted_iota(jnp.int32, exponents.shape, 1)
    exponent = jnp.sum(jnp.where(lane == t, (exponents >> 8) - 128, 0).astype(jnp.float32), 1, keepdims=True)
    return jnp.exp2(exponent) * (1.0 / limit)


def decode(high, low, shift, exponents, t):
    number = high.astype(jnp.int32) * 16 + ((low >> shift) & 15)
    return number.astype(jnp.float32) * unit(exponents, t, FIXED)


def code_kernel(keep, received, code_ref):
    low, _ = encode([keep[:, tile_of(t)] + received[:, tile_of(t)] for t in range(TILES)], code_ref)
    for k in range(LOW):
        code_ref[:, tile_of(TILES + k)] = (low[k] - 32768).astype(jnp.int16)


def sum_kernel(code, pieces, code_ref):
    low = [unsigned(code[:, tile_of(TILES + k)]) for k in range(LOW)]

    def total(t):
        x = decode(code[:, tile_of(t)], low[t // 4], 4 * (t % 4), low[-1], t)
        return jnp.sum(x.reshape(N_Z, HALF // N_Z, LANES), 0)

    out, lane = encode([total(t) for t in range(TILES)], code_ref)
    gram = jnp.sum(pieces[...], 0)
    gram_low = jnp.zeros((HALF // N_Z, LANES), jnp.int32)
    for g in range(2):
        rounded, exponent = fixed_point(gram[:, tile_of(g)], GRAM_FIXED)
        code_ref[:, tile_of(TILES + LOW + 1 + g)] = (rounded >> 8).astype(jnp.int16)
        gram_low = gram_low + ((rounded & 255) << (8 * g))
        out[-1] = out[-1] + jnp.where(lane == TILES + g, exponent << 8, 0)
    for k in range(LOW):
        code_ref[:, tile_of(TILES + k)] = (out[k] - 32768).astype(jnp.int16)
    code_ref[:, tile_of(GRAM_LOW)] = (gram_low - 32768).astype(jnp.int16)


def code_step(keep, received):
    half = pl.BlockSpec((HALF, COLS), lambda t: (0, 0))
    return pl.pallas_call(
        code_kernel,
        grid=(1,),
        in_specs=[half, half],
        out_specs=pl.BlockSpec((HALF, CODE), lambda t: (0, 0)),
        out_shape=jax.ShapeDtypeStruct((HALF, CODE), jnp.int16),
        compiler_params=pltpu.CompilerParams(vmem_limit_bytes=DESIGN_VMEM),
        name="code",
    )(keep, received)


def sum_step(code, pieces):
    vmem = pl.BlockSpec(memory_space=pltpu.VMEM)
    return pl.pallas_call(
        sum_kernel,
        in_specs=[vmem, vmem],
        out_specs=vmem,
        out_shape=jax.ShapeDtypeStruct((HALF // N_Z, WIDE), jnp.int16),
        compiler_params=pltpu.CompilerParams(vmem_limit_bytes=VMEM_LIMIT),
        name="sum",
    )(code, pieces)


FULL = dict(precision=lax.Precision.HIGHEST, preferred_element_type=jnp.float32)


def factor_kernel(high, low, exponents, inv_ref, x_ref, s_ref):
    row = lax.broadcasted_iota(jnp.int32, (PANEL, PANEL), 0)
    col = lax.broadcasted_iota(jnp.int32, (PANEL, PANEL), 1)
    diag = (row == col).astype(jnp.float32)
    phi = jnp.where(row > col, 1.0, 0.5 * diag)
    low_bits = unsigned(low[...])
    exps = unsigned(exponents[...])

    def gram_tile(k):
        number = high[:, tile_of(k)].astype(jnp.int32) * 256 + ((low_bits >> (8 * k)) & 255)
        return number.astype(jnp.float32) * unit(exps, TILES + k, GRAM_FIXED)

    g = jnp.concatenate([gram_tile(0), gram_tile(1)], 1)
    g = jnp.where(row >= col, g, g.T)
    on_diag = g * diag
    d_row = lax.rsqrt(jnp.sum(on_diag, 0, keepdims=True))
    d_col = lax.rsqrt(jnp.sum(on_diag, 1, keepdims=True))
    scaled = g * d_row * d_col
    x = START * (diag - phi * (START * START * scaled - diag))
    low = scaled.astype(jnp.bfloat16)
    for _ in range(2):
        x_low = x.astype(jnp.bfloat16)
        error = nt(nn(x_low, low).astype(jnp.bfloat16), x_low) - diag
        x = x - nn((phi * error).astype(jnp.bfloat16), x_low)
    x_ref[...] = x
    s_ref[...] = scaled

    def more(state):
        step, size = state
        return (step < 12) & (size >= 1e-6) & (size < 1e6)

    def refine(state):
        x = x_ref[...]
        half = lax.dot_general(x, s_ref[...], (((1,), (0,)), ((), ())), **FULL)
        error = lax.dot_general(half, x, (((1,), (1,)), ((), ())), **FULL) - diag
        x_ref[...] = x - nn((phi * error).astype(jnp.bfloat16), x.astype(jnp.bfloat16))
        return state[0] + 1, jnp.sum(error * error)

    _, size = lax.while_loop(more, refine, (0, jnp.float32(1.0)))
    inv_ref[...] = x_ref[...] * d_row

    @pl.when(jnp.logical_not(size < 1e-6))
    def _():
        x_ref[...] = diag
        s_ref[...] = scaled
        index = lax.broadcasted_iota(jnp.int32, (PANEL, 1), 0)
        lane = lax.broadcasted_iota(jnp.int32, (1, PANEL), 1)

        def eliminate(j, carry):
            s = s_ref[...]
            s_row = s_ref[pl.ds(j, 1), :]
            x_row = x_ref[pl.ds(j, 1), :]
            pivot = jnp.sum(jnp.where(lane == j, s_row, 0.0), 1, keepdims=True)
            column = jnp.sum(jnp.where(lane == j, s, 0.0), 1, keepdims=True)
            below = jnp.where(index > j, column / pivot, 0.0)
            s_ref[...] = s - below * s_row
            x = x_ref[...] - below * x_row
            x_ref[...] = jnp.where(index == j, x * lax.rsqrt(pivot), x)
            return carry

        lax.fori_loop(0, PANEL, eliminate, 0)
        inv_ref[...] = x_ref[...] * d_row


def factor_step(code):
    tile = lambda k: pl.BlockSpec((PANEL, LANES), lambda t: (0, k))
    return pl.pallas_call(
        factor_kernel,
        grid=(1,),
        in_specs=[
            pl.BlockSpec((PANEL, PANEL), lambda t: (0, (TILES + LOW + 1) // 2)),
            tile(GRAM_LOW),
            tile(TILES + LOW - 1),
        ],
        out_specs=pl.BlockSpec((PANEL, PANEL), lambda t: (0, 0)),
        out_shape=jax.ShapeDtypeStruct((PANEL, PANEL), jnp.float32),
        scratch_shapes=[pltpu.VMEM((PANEL, PANEL), jnp.float32)] * 2,
        compiler_params=pltpu.CompilerParams(vmem_limit_bytes=VMEM_LIMIT),
        name="factor",
    )(code, code, code)


def update_kernel(
    place, design, high, low, exponents, inverse_factor, panel, updated_ref, coupling_ref, q_ref
):
    t = pl.program_id(0)

    @pl.when(t == 0)
    def _():
        p_hi, p_lo = halves(panel[...])
        f_hi, f_lo = halves(inverse_factor[...])
        q_ref[...] = nt(p_hi, f_hi) + nt(p_hi, f_lo) + nt(p_lo, f_hi)

    @pl.when(t < place[1])
    def _():
        updated_ref[...] = design[...]
        coupling_ref[...] = jnp.zeros((PANEL, TILE), jnp.float32)

    @pl.when(t >= place[1])
    def _():
        f_hi, f_lo = halves(inverse_factor[...])
        low_bits = unsigned(low[...]) >> (8 * lax.rem(t, 2))
        exps = unsigned(exponents[...])
        left = decode(high[:, tile_of(0)], low_bits, 0, exps, 2 * t)
        right = decode(high[:, tile_of(1)], low_bits, 4, exps, 2 * t + 1)
        w_hi, w_lo = halves(jnp.concatenate([left, right], 1))
        coupling = nn(f_hi, w_hi) + nn(f_hi, w_lo) + nn(f_lo, w_hi)
        coupling_ref[...] = coupling
        q_hi, q_lo = halves(q_ref[...])
        c_hi, c_lo = halves(coupling)
        updated_ref[...] = design[...] - (nn(q_hi, c_hi) + nn(q_hi, c_lo) + nn(q_lo, c_hi))

    @pl.when(t == place[1])
    def _():
        updated_ref[...] = q_ref[...]


def update_step(place, design, code, inverse_factor, panel):
    return pl.pallas_call(
        update_kernel,
        grid_spec=pltpu.PrefetchScalarGridSpec(
            num_scalar_prefetch=1,
            grid=(SLOTS,),
            in_specs=[
                pl.BlockSpec((ROWS, TILE), lambda t, s: (0, t)),
                pl.BlockSpec((PANEL, TILE), lambda t, s: (0, t)),
                pl.BlockSpec((PANEL, LANES), lambda t, s: (0, TILES + t // 2)),
                pl.BlockSpec((PANEL, LANES), lambda t, s: (0, TILES + LOW - 1)),
                pl.BlockSpec((PANEL, PANEL), lambda t, s: (0, 0)),
                pl.BlockSpec((ROWS, PANEL), lambda t, s: (0, 0)),
            ],
            out_specs=(
                pl.BlockSpec((ROWS, TILE), lambda t, s: (0, t)),
                pl.BlockSpec((PANEL, TILE), lambda t, s: (0, t)),
            ),
            scratch_shapes=[pltpu.VMEM((ROWS, PANEL), jnp.float32)],
        ),
        out_shape=(
            jax.ShapeDtypeStruct((ROWS, COLS), jnp.float32),
            jax.ShapeDtypeStruct((PANEL, COLS), jnp.float32),
        ),
        compiler_params=pltpu.CompilerParams(vmem_limit_bytes=VMEM_LIMIT),
        name="update",
    )(place, design, code, code, code, inverse_factor, panel)


def shards(env_desc, env_counts, reg_desc, sparse_desc, panel_block):
    core = lax.axis_index("env") % 2
    column_shard = lax.axis_index("sp")
    owner = panel_block // SLOTS

    gathered = lax.all_gather(sparse_desc, "env", axis=1, tiled=True)

    with jax.named_scope("panel_points"):
        mine = lax.dynamic_index_in_dim(sparse_desc, panel_block - owner * SLOTS, 0, keepdims=False)
        offered = jnp.broadcast_to(mine[None], (N_SP,) + mine.shape)
        offered = lax.all_to_all(offered, "sp", 0, 0)
        mine = lax.dynamic_index_in_dim(offered, owner, 0, keepdims=False)
        panel_points = lax.all_gather(mine, "env", axis=0, tiled=True)

    counts = env_counts[0]
    finish = jnp.cumsum(counts)
    starts = finish - counts
    inverse = 1.0 / counts.astype(jnp.float32)
    place = jnp.stack([core, panel_block - column_shard * SLOTS]).astype(jnp.int32)
    panel, panel_hi, panel_lo, gram, member = panel_step(
        panel_points, env_desc, reg_desc, starts[:, None], finish[:, None], inverse[None, :]
    )

    with jax.named_scope("gram"):
        pieces = gram.reshape(2 * N_Z, HALF // N_Z, PANEL)
        pieces = lax.all_to_all(pieces, "env", 0, 0)

    points = gathered.reshape(COLS, DESC)
    design, keep, send = design_step(
        place, points, env_desc, reg_desc, member, inverse[:, None], panel_hi, panel_lo
    )

    with jax.named_scope("product"):
        send, pieces = lax.optimization_barrier((send, pieces))
        code = code_step(keep, lax.ppermute(send, "env", CORE_SWAP))
        code = code.reshape(N_Z, HALF // N_Z, CODE)
        code = lax.all_to_all(code, "env", 0, 0, axis_index_groups=SAME_CORE)
        code = sum_step(code.reshape(HALF, CODE), pieces)
        code = lax.all_gather(code, "env", axis=0, tiled=True)

    return update_step(place, design, code, factor_step(code), panel)


def solution(mesh):
    in_specs = (P("env", None), P("env", None), P("env", None), P("sp", "env", None), P())
    out_specs = (P("env", "sp"), P(None, "sp"))
    return jax.shard_map(shards, mesh=mesh, in_specs=in_specs, out_specs=out_specs, check_vma=False)
```

```python
import jax
import jax.numpy as jnp
from jax import lax
from jax.experimental import pallas as pl
from jax.experimental.pallas import tpu as pltpu
from jax.sharding import PartitionSpec as P

DESC = 1000
PANEL = 256
TILE = 256
N_Z = 16
N_SP = 16
CONF = 448
ENV = 1024
REG = 64
ROWS = CONF + REG
SLOTS = 5
COLS = SLOTS * PANEL
HALF = PANEL // 2
START = 0.95
BLOCK = HALF // 4
GRAM_ROWS = 8
LANES = 128
TILES = COLS // LANES
LOW = 3
CODE = (TILES + LOW) * LANES
FIXED = 524286.0
GRAM_FIXED = 8388606.0
WIDE = CODE + 3 * LANES
GRAM_LOW = TILES + LOW

cube_scale = 15.0 ** (-0.5)
dot_scale = DESC ** (-0.5)
VMEM_LIMIT = 40 * 1024 * 1024
DESIGN_VMEM = 60 * 1024 * 1024

NEAR = [[2 * (4 * j + r) + c for r in range(4)] for j in range(4) for c in range(2)]
FAR = [[2 * (4 * j + r) + c for j in range(4)] for r in range(4) for c in range(2)]
CHIPS = [[8 * j + i for i in range(8)] for j in range(4)]
CORE_SWAP = [(i, i ^ 1) for i in range(2 * N_Z)]


def nt(a, b):
    return lax.dot_general(a, b, (((1,), (1,)), ((), ())), preferred_element_type=jnp.float32)


def nn(a, b):
    return lax.dot_general(a, b, (((1,), (0,)), ((), ())), preferred_element_type=jnp.float32)


def halves(x):
    hi = x.astype(jnp.bfloat16)
    lo = (x - hi.astype(jnp.float32)).astype(jnp.bfloat16)
    return hi, lo


def cubed(product):
    scaled = product * dot_scale
    return scaled * scaled * scaled * cube_scale


def panel_kernel(points, env, reg, starts, finish, inverse, panel_ref, hi_ref, lo_ref, gram_ref, member_ref):
    position = lax.broadcasted_iota(jnp.int32, (CONF, ENV), 1)
    inside = (position >= starts[...]) & (position < finish[...])
    member = inside.astype(jnp.float32).astype(jnp.bfloat16)
    member_ref[...] = member
    pts = points[...]
    hi, lo = halves(cubed(nt(pts, env[...])))
    energy = (nt(hi, member) + nt(lo, member)) * inverse[...]
    panel_t = jnp.concatenate([energy, cubed(nt(pts, reg[...]))], 1)
    panel_ref[...] = panel_t.T
    hi, lo = halves(panel_t)
    hi_ref[...] = hi
    lo_ref[...] = lo
    gram_ref[...] = lax.dot_general(
        panel_t,
        panel_t,
        (((1,), (1,)), ((), ())),
        precision=lax.Precision.HIGHEST,
        preferred_element_type=jnp.float32,
    )


def panel_step(points, env, reg, starts, finish, inverse):
    return pl.pallas_call(
        panel_kernel,
        out_shape=(
            jax.ShapeDtypeStruct((ROWS, PANEL), jnp.float32),
            jax.ShapeDtypeStruct((PANEL, ROWS), jnp.bfloat16),
            jax.ShapeDtypeStruct((PANEL, ROWS), jnp.bfloat16),
            jax.ShapeDtypeStruct((PANEL, PANEL), jnp.float32),
            jax.ShapeDtypeStruct((CONF, ENV), jnp.bfloat16),
        ),
        compiler_params=pltpu.CompilerParams(vmem_limit_bytes=VMEM_LIMIT),
        name="panel",
    )(points, env, reg, starts, finish, inverse)


def design_kernel(
    place, points, env, reg, member, inverse, panel_hi, panel_lo, design_ref, keep_ref, send_ref, rows_ref, sem
):
    pts = points[...]
    hi, lo = halves(cubed(nt(env[...], pts)))
    weights = member[...]
    rows_ref[:CONF] = (nn(weights, hi) + nn(weights, lo)) * inverse[...]
    rows_ref[CONF:] = cubed(nt(reg[...], pts))
    leave = pltpu.make_async_copy(rows_ref, design_ref, sem)
    leave.start()
    hi, lo = halves(rows_ref[...])
    left = panel_hi[...]
    product = nn(left, hi) + nn(left, lo) + nn(panel_lo[...], hi)
    product = product.reshape(4, 2, BLOCK, COLS)
    first = place[0] == 0
    keep_ref[...] = jnp.where(first, product[:, 0], product[:, 1]).reshape(HALF, COLS)
    send_ref[...] = jnp.where(first, product[:, 1], product[:, 0]).reshape(HALF, COLS)
    leave.wait()


def design_step(place, points, env, reg, member, inverse, panel_hi, panel_lo):
    half = pl.BlockSpec((HALF, COLS), lambda t, s: (0, 0))
    arrays = (points, env, reg, member, inverse, panel_hi, panel_lo)
    return pl.pallas_call(
        design_kernel,
        grid_spec=pltpu.PrefetchScalarGridSpec(
            num_scalar_prefetch=1,
            grid=(1,),
            in_specs=[pl.BlockSpec(a.shape, lambda t, s: (0, 0)) for a in arrays],
            out_specs=(pl.BlockSpec(memory_space=pl.ANY), half, half),
            scratch_shapes=[pltpu.VMEM((ROWS, COLS), jnp.float32), pltpu.SemaphoreType.DMA],
        ),
        out_shape=(
            jax.ShapeDtypeStruct((ROWS, COLS), jnp.float32),
            jax.ShapeDtypeStruct((HALF, COLS), jnp.float32),
            jax.ShapeDtypeStruct((HALF, COLS), jnp.float32),
        ),
        compiler_params=pltpu.CompilerParams(vmem_limit_bytes=DESIGN_VMEM),
        cost_estimate=pl.CostEstimate(flops=7 * 10**9, bytes_accessed=9 * 10**6, transcendentals=0),
        name="design",
    )(place, *arrays)


def tile_of(t):
    return slice(t * LANES, (t + 1) * LANES)


def fixed_point(x, limit):
    largest = jnp.maximum(jnp.max(jnp.abs(x), 1, keepdims=True), 1e-30)
    exponent = jnp.minimum(jnp.ceil(jnp.log2(largest) + 1e-4), 127.0)
    scaled = jnp.clip(x * (jnp.exp2(-exponent) * limit), -limit, limit)
    return jnp.where(scaled < 0, scaled - 0.5, scaled + 0.5).astype(jnp.int32), exponent.astype(jnp.int32) + 128


def encode(tiles, code_ref):
    rows = code_ref.shape[0]
    lane = lax.broadcasted_iota(jnp.int32, (rows, LANES), 1)
    low = [jnp.zeros((rows, LANES), jnp.int32) for _ in range(LOW)]
    for t, x in enumerate(tiles):
        rounded, exponent = fixed_point(x, FIXED)
        code_ref[:, tile_of(t)] = (rounded >> 4).astype(jnp.int16)
        low[t // 4] = low[t // 4] + ((rounded & 15) << (4 * (t % 4)))
        low[-1] = low[-1] + jnp.where(lane == t, exponent << 8, 0)
    return low, lane


def unsigned(code):
    return code.astype(jnp.int32) + 32768


def unit(exponents, t, limit):
    lane = lax.broadcasted_iota(jnp.int32, exponents.shape, 1)
    exponent = jnp.sum(jnp.where(lane == t, (exponents >> 8) - 128, 0).astype(jnp.float32), 1, keepdims=True)
    return jnp.exp2(exponent) * (1.0 / limit)


def decode(high, low, shift, exponents, t):
    number = high.astype(jnp.int32) * 16 + ((low >> shift) & 15)
    return number.astype(jnp.float32) * unit(exponents, t, FIXED)


def code_kernel(keep, received, code_ref):
    low, _ = encode([keep[:, tile_of(t)] + received[:, tile_of(t)] for t in range(TILES)], code_ref)
    for k in range(LOW):
        code_ref[:, tile_of(TILES + k)] = (low[k] - 32768).astype(jnp.int16)


def quarter_sums(code):
    low = [unsigned(code[:, tile_of(TILES + k)]) for k in range(LOW)]
    tiles = []
    for t in range(TILES):
        x = decode(code[:, tile_of(t)], low[t // 4], 4 * (t % 4), low[-1], t)
        tiles.append(jnp.sum(x.reshape(4, BLOCK, LANES), 0))
    return tiles


def near_kernel(code, pieces, code_ref):
    out, lane = encode(quarter_sums(code), code_ref)
    rest = jnp.zeros((BLOCK - GRAM_ROWS, LANES), jnp.int32)
    gram = jnp.sum(pieces[...], 0)
    gram_low = jnp.zeros((GRAM_ROWS, LANES), jnp.int32)
    for g in range(2):
        rounded, exponent = fixed_point(gram[:, tile_of(g)], GRAM_FIXED)
        high = jnp.concatenate([rounded >> 8, rest], 0)
        code_ref[:, tile_of(GRAM_LOW + 1 + g)] = high.astype(jnp.int16)
        gram_low = gram_low + ((rounded & 255) << (8 * g))
        exponents = jnp.where(lane[:GRAM_ROWS] == TILES + g, exponent << 8, 0)
        out[-1] = out[-1] + jnp.concatenate([exponents, rest], 0)
    for k in range(LOW):
        code_ref[:, tile_of(TILES + k)] = (out[k] - 32768).astype(jnp.int16)
    code_ref[:, tile_of(GRAM_LOW)] = (jnp.concatenate([gram_low, rest], 0) - 32768).astype(jnp.int16)


def far_kernel(code, code_ref):
    out, lane = encode(quarter_sums(code), code_ref)

    def gram_rows(x):
        return jnp.concatenate([x[BLOCK * j : BLOCK * j + GRAM_ROWS] for j in range(4)], 0)

    for k in range(3):
        tile = tile_of(GRAM_LOW + k)
        code_ref[:, tile] = gram_rows(code[:, tile].astype(jnp.int32)).astype(jnp.int16)
    exponents = gram_rows((unsigned(code[:, tile_of(TILES + LOW - 1)]) >> 8) << 8)
    out[-1] = out[-1] + jnp.where((lane == TILES) | (lane == TILES + 1), exponents, 0)
    for k in range(LOW):
        code_ref[:, tile_of(TILES + k)] = (out[k] - 32768).astype(jnp.int16)


def code_step(keep, received):
    vmem = pl.BlockSpec(memory_space=pltpu.VMEM)
    return pl.pallas_call(
        code_kernel,
        in_specs=[vmem, vmem],
        out_specs=vmem,
        out_shape=jax.ShapeDtypeStruct((HALF, CODE), jnp.int16),
        compiler_params=pltpu.CompilerParams(vmem_limit_bytes=VMEM_LIMIT),
        name="code",
    )(keep, received)


def sum_step(kernel, *arrays):
    vmem = pl.BlockSpec(memory_space=pltpu.VMEM)
    return pl.pallas_call(
        kernel,
        in_specs=[vmem] * len(arrays),
        out_specs=vmem,
        out_shape=jax.ShapeDtypeStruct((BLOCK, WIDE), jnp.int16),
        compiler_params=pltpu.CompilerParams(vmem_limit_bytes=VMEM_LIMIT),
        name="sum",
    )(*arrays)


FULL = dict(precision=lax.Precision.HIGHEST, preferred_element_type=jnp.float32)


def factor_kernel(high, low, exponents, inv_ref, x_ref, s_ref):
    row = lax.broadcasted_iota(jnp.int32, (PANEL, PANEL), 0)
    col = lax.broadcasted_iota(jnp.int32, (PANEL, PANEL), 1)
    diag = (row == col).astype(jnp.float32)
    phi = jnp.where(row > col, 1.0, 0.5 * diag)
    low_bits = unsigned(low[...])
    exps = unsigned(exponents[...])

    def gram_tile(k):
        number = high[:, tile_of(k)].astype(jnp.int32) * 256 + ((low_bits >> (8 * k)) & 255)
        return number.astype(jnp.float32) * unit(exps, TILES + k, GRAM_FIXED)

    g = jnp.concatenate([gram_tile(0), gram_tile(1)], 1)
    g = jnp.where(row >= col, g, g.T)
    on_diag = g * diag
    d_row = lax.rsqrt(jnp.sum(on_diag, 0, keepdims=True))
    d_col = lax.rsqrt(jnp.sum(on_diag, 1, keepdims=True))
    scaled = g * d_row * d_col
    x = START * (diag - phi * (START * START * scaled - diag))
    low = scaled.astype(jnp.bfloat16)
    for _ in range(2):
        x_low = x.astype(jnp.bfloat16)
        error = nt(nn(x_low, low).astype(jnp.bfloat16), x_low) - diag
        x = x - nn((phi * error).astype(jnp.bfloat16), x_low)
    x_ref[...] = x
    s_ref[...] = scaled

    def more(state):
        step, size = state
        return (step < 12) & (size >= 1e-6) & (size < 1e6)

    def refine(state):
        x = x_ref[...]
        half = lax.dot_general(x, s_ref[...], (((1,), (0,)), ((), ())), **FULL)
        error = lax.dot_general(half, x, (((1,), (1,)), ((), ())), **FULL) - diag
        x_ref[...] = x - nn((phi * error).astype(jnp.bfloat16), x.astype(jnp.bfloat16))
        return state[0] + 1, jnp.sum(error * error)

    _, size = lax.while_loop(more, refine, (0, jnp.float32(1.0)))
    inv_ref[...] = x_ref[...] * d_row

    @pl.when(jnp.logical_not(size < 1e-6))
    def _():
        x_ref[...] = diag
        s_ref[...] = scaled
        index = lax.broadcasted_iota(jnp.int32, (PANEL, 1), 0)
        lane = lax.broadcasted_iota(jnp.int32, (1, PANEL), 1)

        def eliminate(j, carry):
            s = s_ref[...]
            s_row = s_ref[pl.ds(j, 1), :]
            x_row = x_ref[pl.ds(j, 1), :]
            pivot = jnp.sum(jnp.where(lane == j, s_row, 0.0), 1, keepdims=True)
            column = jnp.sum(jnp.where(lane == j, s, 0.0), 1, keepdims=True)
            below = jnp.where(index > j, column / pivot, 0.0)
            s_ref[...] = s - below * s_row
            x = x_ref[...] - below * x_row
            x_ref[...] = jnp.where(index == j, x * lax.rsqrt(pivot), x)
            return carry

        lax.fori_loop(0, PANEL, eliminate, 0)
        inv_ref[...] = x_ref[...] * d_row


def factor_step(code):
    tile = lambda k: pl.BlockSpec((PANEL, LANES), lambda t: (0, k))
    return pl.pallas_call(
        factor_kernel,
        grid=(1,),
        in_specs=[
            pl.BlockSpec((PANEL, PANEL), lambda t: (0, (TILES + LOW + 1) // 2)),
            tile(GRAM_LOW),
            tile(TILES + LOW - 1),
        ],
        out_specs=pl.BlockSpec((PANEL, PANEL), lambda t: (0, 0)),
        out_shape=jax.ShapeDtypeStruct((PANEL, PANEL), jnp.float32),
        scratch_shapes=[pltpu.VMEM((PANEL, PANEL), jnp.float32)] * 2,
        compiler_params=pltpu.CompilerParams(vmem_limit_bytes=VMEM_LIMIT),
        name="factor",
    )(code, code, code)


def update_kernel(
    place, design, high, low, exponents, inverse_factor, panel, updated_ref, coupling_ref, q_ref
):
    t = pl.program_id(0)

    @pl.when(t == 0)
    def _():
        p_hi, p_lo = halves(panel[...])
        f_hi, f_lo = halves(inverse_factor[...])
        q_ref[...] = nt(p_hi, f_hi) + nt(p_hi, f_lo) + nt(p_lo, f_hi)

    @pl.when(t < place[1])
    def _():
        updated_ref[...] = design[...]
        coupling_ref[...] = jnp.zeros((PANEL, TILE), jnp.float32)

    @pl.when(t >= place[1])
    def _():
        f_hi, f_lo = halves(inverse_factor[...])
        low_bits = unsigned(low[...]) >> (8 * lax.rem(t, 2))
        exps = unsigned(exponents[...])
        left = decode(high[:, tile_of(0)], low_bits, 0, exps, 2 * t)
        right = decode(high[:, tile_of(1)], low_bits, 4, exps, 2 * t + 1)
        w_hi, w_lo = halves(jnp.concatenate([left, right], 1))
        coupling = nn(f_hi, w_hi) + nn(f_hi, w_lo) + nn(f_lo, w_hi)
        coupling_ref[...] = coupling
        q_hi, q_lo = halves(q_ref[...])
        c_hi, c_lo = halves(coupling)
        updated_ref[...] = design[...] - (nn(q_hi, c_hi) + nn(q_hi, c_lo) + nn(q_lo, c_hi))

    @pl.when(t == place[1])
    def _():
        updated_ref[...] = q_ref[...]


def update_step(place, design, code, inverse_factor, panel):
    return pl.pallas_call(
        update_kernel,
        grid_spec=pltpu.PrefetchScalarGridSpec(
            num_scalar_prefetch=1,
            grid=(SLOTS,),
            in_specs=[
                pl.BlockSpec((ROWS, TILE), lambda t, s: (0, t)),
                pl.BlockSpec((PANEL, TILE), lambda t, s: (0, t)),
                pl.BlockSpec((PANEL, LANES), lambda t, s: (0, TILES + t // 2)),
                pl.BlockSpec((PANEL, LANES), lambda t, s: (0, TILES + LOW - 1)),
                pl.BlockSpec((PANEL, PANEL), lambda t, s: (0, 0)),
                pl.BlockSpec((ROWS, PANEL), lambda t, s: (0, 0)),
            ],
            out_specs=(
                pl.BlockSpec((ROWS, TILE), lambda t, s: (0, t)),
                pl.BlockSpec((PANEL, TILE), lambda t, s: (0, t)),
            ),
            scratch_shapes=[pltpu.VMEM((ROWS, PANEL), jnp.float32)],
        ),
        out_shape=(
            jax.ShapeDtypeStruct((ROWS, COLS), jnp.float32),
            jax.ShapeDtypeStruct((PANEL, COLS), jnp.float32),
        ),
        compiler_params=pltpu.CompilerParams(vmem_limit_bytes=VMEM_LIMIT),
        name="update",
    )(place, design, code, code, code, inverse_factor, panel)


def shards(env_desc, env_counts, reg_desc, sparse_desc, panel_block):
    core = lax.axis_index("env") % 2
    column_shard = lax.axis_index("sp")
    owner = panel_block // SLOTS

    gathered = lax.all_gather(sparse_desc, "env", axis=1, tiled=True)

    with jax.named_scope("panel_points"):
        mine = lax.dynamic_index_in_dim(sparse_desc, panel_block - owner * SLOTS, 0, keepdims=False)
        offered = jnp.broadcast_to(mine[None], (N_SP,) + mine.shape)
        offered = lax.all_to_all(offered, "sp", 0, 0)
        mine = lax.dynamic_index_in_dim(offered, owner, 0, keepdims=False)
        panel_points = lax.all_gather(mine, "env", axis=0, tiled=True)

    counts = env_counts[0]
    finish = jnp.cumsum(counts)
    starts = finish - counts
    inverse = 1.0 / counts.astype(jnp.float32)
    place = jnp.stack([core, panel_block - column_shard * SLOTS]).astype(jnp.int32)
    panel, panel_hi, panel_lo, gram, member = panel_step(
        panel_points, env_desc, reg_desc, starts[:, None], finish[:, None], inverse[None, :]
    )

    with jax.named_scope("gram"):
        pieces = gram.reshape(4, 2, 4, GRAM_ROWS, PANEL).transpose(2, 0, 1, 3, 4)
        pieces = pieces.reshape(2 * N_Z, GRAM_ROWS, PANEL)
        pieces = lax.all_to_all(pieces, "env", 0, 0)

    points = gathered.reshape(COLS, DESC)
    design, keep, send = design_step(
        place, points, env_desc, reg_desc, member, inverse[:, None], panel_hi, panel_lo
    )

    with jax.named_scope("product"):
        send, pieces = lax.optimization_barrier((send, pieces))
        code = code_step(keep, lax.ppermute(send, "env", CORE_SWAP))
        code = code.reshape(4, BLOCK, CODE)
        code = lax.all_to_all(code, "env", 0, 0, axis_index_groups=NEAR)
        code = sum_step(near_kernel, code.reshape(HALF, CODE), pieces)
        code = lax.all_gather(code, "env", axis=0, tiled=True, axis_index_groups=FAR)
        code = sum_step(far_kernel, code)
        code = lax.all_gather(code, "env", axis=0, tiled=True, axis_index_groups=CHIPS)

    return update_step(place, design, code, factor_step(code), panel)


def solution(mesh):
    in_specs = (P("env", None), P("env", None), P("env", None), P("sp", "env", None), P())
    out_specs = (P("env", "sp"), P(None, "sp"))
    return jax.shard_map(shards, mesh=mesh, in_specs=in_specs, out_specs=out_specs, check_vma=False)
```

```python
import jax
import jax.numpy as jnp
from jax import lax
from jax.experimental import pallas as pl
from jax.experimental.pallas import tpu as pltpu
from jax.sharding import PartitionSpec as P

DESC = 1000
PANEL = 256
TILE = 256
N_Z = 16
N_SP = 16
CONF = 448
ENV = 1024
REG = 64
ROWS = CONF + REG
SLOTS = 5
COLS = SLOTS * PANEL
HALF = PANEL // 2
START = 0.95
BLOCK = HALF // 4
GRAM_ROWS = 8
LANES = 128
TILES = COLS // LANES
LOW = 3
CODE = (TILES + LOW) * LANES
FIXED = 524286.0
GRAM_FIXED = 8388606.0
WIDE = CODE + 3 * LANES
GRAM_LOW = TILES + LOW

cube_scale = 15.0 ** (-0.5)
dot_scale = DESC ** (-0.5)
VMEM_LIMIT = 40 * 1024 * 1024
DESIGN_VMEM = 60 * 1024 * 1024

NEAR = [[2 * (4 * j + r) + c for r in range(4)] for j in range(4) for c in range(2)]
FAR = [[2 * (4 * j + r) + c for j in range(4)] for r in range(4) for c in range(2)]
CHIPS = [[8 * j + i for i in range(8)] for j in range(4)]
CORE_SWAP = [(i, i ^ 1) for i in range(2 * N_Z)]


def nt(a, b):
    return lax.dot_general(a, b, (((1,), (1,)), ((), ())), preferred_element_type=jnp.float32)


def nn(a, b):
    return lax.dot_general(a, b, (((1,), (0,)), ((), ())), preferred_element_type=jnp.float32)


def halves(x):
    hi = x.astype(jnp.bfloat16)
    lo = (x - hi.astype(jnp.float32)).astype(jnp.bfloat16)
    return hi, lo


def cubed(product):
    scaled = product * dot_scale
    return scaled * scaled * scaled * cube_scale


def panel_kernel(points, env, reg, starts, finish, inverse, panel_ref, hi_ref, lo_ref, gram_ref, member_ref):
    position = lax.broadcasted_iota(jnp.int32, (CONF, ENV), 1)
    inside = (position >= starts[...]) & (position < finish[...])
    member = inside.astype(jnp.float32).astype(jnp.bfloat16)
    member_ref[...] = member
    pts = points[...]
    hi, lo = halves(cubed(nt(pts, env[...])))
    energy = (nt(hi, member) + nt(lo, member)) * inverse[...]
    panel_t = jnp.concatenate([energy, cubed(nt(pts, reg[...]))], 1)
    panel_ref[...] = panel_t.T
    hi, lo = halves(panel_t)
    hi_ref[...] = hi
    lo_ref[...] = lo
    gram_ref[...] = lax.dot_general(
        panel_t,
        panel_t,
        (((1,), (1,)), ((), ())),
        precision=lax.Precision.HIGHEST,
        preferred_element_type=jnp.float32,
    )


def panel_step(points, env, reg, starts, finish, inverse):
    return pl.pallas_call(
        panel_kernel,
        out_shape=(
            jax.ShapeDtypeStruct((ROWS, PANEL), jnp.float32),
            jax.ShapeDtypeStruct((PANEL, ROWS), jnp.bfloat16),
            jax.ShapeDtypeStruct((PANEL, ROWS), jnp.bfloat16),
            jax.ShapeDtypeStruct((PANEL, PANEL), jnp.float32),
            jax.ShapeDtypeStruct((CONF, ENV), jnp.bfloat16),
        ),
        compiler_params=pltpu.CompilerParams(vmem_limit_bytes=VMEM_LIMIT),
        name="panel",
    )(points, env, reg, starts, finish, inverse)


def design_kernel(
    place, points, env, reg, member, inverse, panel_hi, panel_lo, design_ref, keep_ref, send_ref, rows_ref, sem
):
    pts = points[...]
    hi, lo = halves(cubed(nt(env[...], pts)))
    weights = member[...]
    rows_ref[:CONF] = (nn(weights, hi) + nn(weights, lo)) * inverse[...]
    rows_ref[CONF:] = cubed(nt(reg[...], pts))
    leave = pltpu.make_async_copy(rows_ref, design_ref, sem)
    leave.start()
    hi, lo = halves(rows_ref[...])
    left = panel_hi[...]
    product = nn(left, hi) + nn(left, lo) + nn(panel_lo[...], hi)
    product = product.reshape(4, 2, BLOCK, COLS)
    first = place[0] == 0
    keep_ref[...] = jnp.where(first, product[:, 0], product[:, 1]).reshape(HALF, COLS)
    send_ref[...] = jnp.where(first, product[:, 1], product[:, 0]).reshape(HALF, COLS)
    leave.wait()


def design_step(place, points, env, reg, member, inverse, panel_hi, panel_lo):
    half = pl.BlockSpec((HALF, COLS), lambda t, s: (0, 0))
    arrays = (points, env, reg, member, inverse, panel_hi, panel_lo)
    return pl.pallas_call(
        design_kernel,
        grid_spec=pltpu.PrefetchScalarGridSpec(
            num_scalar_prefetch=1,
            grid=(1,),
            in_specs=[pl.BlockSpec(a.shape, lambda t, s: (0, 0)) for a in arrays],
            out_specs=(pl.BlockSpec(memory_space=pl.ANY), half, half),
            scratch_shapes=[pltpu.VMEM((ROWS, COLS), jnp.float32), pltpu.SemaphoreType.DMA],
        ),
        out_shape=(
            jax.ShapeDtypeStruct((ROWS, COLS), jnp.float32),
            jax.ShapeDtypeStruct((HALF, COLS), jnp.float32),
            jax.ShapeDtypeStruct((HALF, COLS), jnp.float32),
        ),
        compiler_params=pltpu.CompilerParams(vmem_limit_bytes=DESIGN_VMEM),
        cost_estimate=pl.CostEstimate(flops=7 * 10**9, bytes_accessed=9 * 10**6, transcendentals=0),
        name="design",
    )(place, *arrays)


def tile_of(t):
    return slice(t * LANES, (t + 1) * LANES)


def fixed_point(x, limit):
    largest = jnp.maximum(jnp.max(jnp.abs(x), 1, keepdims=True), 1e-30)
    exponent = jnp.minimum(jnp.ceil(jnp.log2(largest) + 1e-4), 127.0)
    scaled = jnp.clip(x * (jnp.exp2(-exponent) * limit), -limit, limit)
    return jnp.where(scaled < 0, scaled - 0.5, scaled + 0.5).astype(jnp.int32), exponent.astype(jnp.int32) + 128


def encode(tiles, code_ref):
    rows = code_ref.shape[0]
    lane = lax.broadcasted_iota(jnp.int32, (rows, LANES), 1)
    low = [jnp.zeros((rows, LANES), jnp.int32) for _ in range(LOW)]
    for t, x in enumerate(tiles):
        rounded, exponent = fixed_point(x, FIXED)
        code_ref[:, tile_of(t)] = (rounded >> 4).astype(jnp.int16)
        low[t // 4] = low[t // 4] + ((rounded & 15) << (4 * (t % 4)))
        low[-1] = low[-1] + jnp.where(lane == t, exponent << 8, 0)
    return low, lane


def unsigned(code):
    return code.astype(jnp.int32) + 32768


def unit(exponents, t, limit):
    lane = lax.broadcasted_iota(jnp.int32, exponents.shape, 1)
    exponent = jnp.sum(jnp.where(lane == t, (exponents >> 8) - 128, 0).astype(jnp.float32), 1, keepdims=True)
    return jnp.exp2(exponent) * (1.0 / limit)


def decode(high, low, shift, exponents, t):
    number = high.astype(jnp.int32) * 16 + ((low >> shift) & 15)
    return number.astype(jnp.float32) * unit(exponents, t, FIXED)


def code_kernel(keep, received, code_ref):
    low, _ = encode([keep[:, tile_of(t)] + received[:, tile_of(t)] for t in range(TILES)], code_ref)
    for k in range(LOW):
        code_ref[:, tile_of(TILES + k)] = (low[k] - 32768).astype(jnp.int16)


def quarter_sums(code):
    low = [unsigned(code[:, tile_of(TILES + k)]) for k in range(LOW)]
    tiles = []
    for t in range(TILES):
        x = decode(code[:, tile_of(t)], low[t // 4], 4 * (t % 4), low[-1], t)
        tiles.append(jnp.sum(x.reshape(4, BLOCK, LANES), 0))
    return tiles


def near_kernel(code, pieces, code_ref):
    out, lane = encode(quarter_sums(code), code_ref)
    rest = jnp.zeros((BLOCK - GRAM_ROWS, LANES), jnp.int32)
    gram = jnp.sum(pieces[...], 0)
    groups = []
    gram_low = jnp.zeros((GRAM_ROWS, LANES), jnp.int32)
    for g in range(2):
        rounded, exponent = fixed_point(gram[:, tile_of(g)], GRAM_FIXED)
        groups.append(rounded >> 8)
        gram_low = gram_low + ((rounded & 255) << (8 * g))
        exponents = jnp.where(lane[:GRAM_ROWS] == TILES + g, exponent << 8, 0)
        out[-1] = out[-1] + jnp.concatenate([exponents, rest], 0)
    for k in range(LOW):
        code_ref[:, tile_of(TILES + k)] = (out[k] - 32768).astype(jnp.int16)
    groups = [gram_low - 32768] + groups + [rest[:GRAM_ROWS]]
    code_ref[:, tile_of(GRAM_LOW)] = jnp.concatenate(groups, 0).astype(jnp.int16)


def far_kernel(code, code_ref):
    out, lane = encode(quarter_sums(code), code_ref)

    def gram_rows(x, k):
        first = [BLOCK * j + GRAM_ROWS * k for j in range(4)]
        return jnp.concatenate([x[i : i + GRAM_ROWS] for i in first], 0)

    for k in range(3):
        tile = code[:, tile_of(GRAM_LOW)].astype(jnp.int32)
        code_ref[:, tile_of(GRAM_LOW + k)] = gram_rows(tile, k).astype(jnp.int16)
    exponents = gram_rows((unsigned(code[:, tile_of(TILES + LOW - 1)]) >> 8) << 8, 0)
    out[-1] = out[-1] + jnp.where((lane == TILES) | (lane == TILES + 1), exponents, 0)
    for k in range(LOW):
        code_ref[:, tile_of(TILES + k)] = (out[k] - 32768).astype(jnp.int16)


def code_step(keep, received):
    vmem = pl.BlockSpec(memory_space=pltpu.VMEM)
    return pl.pallas_call(
        code_kernel,
        in_specs=[vmem, vmem],
        out_specs=vmem,
        out_shape=jax.ShapeDtypeStruct((HALF, CODE), jnp.int16),
        compiler_params=pltpu.CompilerParams(vmem_limit_bytes=VMEM_LIMIT),
        name="code",
    )(keep, received)


def sum_step(kernel, width, *arrays):
    vmem = pl.BlockSpec(memory_space=pltpu.VMEM)
    return pl.pallas_call(
        kernel,
        in_specs=[vmem] * len(arrays),
        out_specs=vmem,
        out_shape=jax.ShapeDtypeStruct((BLOCK, width), jnp.int16),
        compiler_params=pltpu.CompilerParams(vmem_limit_bytes=VMEM_LIMIT),
        name="sum",
    )(*arrays)


FULL = dict(precision=lax.Precision.HIGHEST, preferred_element_type=jnp.float32)


def factor_kernel(high, low, exponents, inv_ref, x_ref, s_ref):
    row = lax.broadcasted_iota(jnp.int32, (PANEL, PANEL), 0)
    col = lax.broadcasted_iota(jnp.int32, (PANEL, PANEL), 1)
    diag = (row == col).astype(jnp.float32)
    phi = jnp.where(row > col, 1.0, 0.5 * diag)
    low_bits = unsigned(low[...])
    exps = unsigned(exponents[...])

    def gram_tile(k):
        number = high[:, tile_of(k)].astype(jnp.int32) * 256 + ((low_bits >> (8 * k)) & 255)
        return number.astype(jnp.float32) * unit(exps, TILES + k, GRAM_FIXED)

    g = jnp.concatenate([gram_tile(0), gram_tile(1)], 1)
    g = jnp.where(row >= col, g, g.T)
    on_diag = g * diag
    d_row = lax.rsqrt(jnp.sum(on_diag, 0, keepdims=True))
    d_col = lax.rsqrt(jnp.sum(on_diag, 1, keepdims=True))
    scaled = g * d_row * d_col
    x = START * (diag - phi * (START * START * scaled - diag))
    low = scaled.astype(jnp.bfloat16)
    for _ in range(2):
        x_low = x.astype(jnp.bfloat16)
        error = nt(nn(x_low, low).astype(jnp.bfloat16), x_low) - diag
        x = x - nn((phi * error).astype(jnp.bfloat16), x_low)
    x_ref[...] = x
    s_ref[...] = scaled

    def more(state):
        step, size = state
        return (step < 12) & (size >= 1e-6) & (size < 1e6)

    def refine(state):
        x = x_ref[...]
        half = lax.dot_general(x, s_ref[...], (((1,), (0,)), ((), ())), **FULL)
        error = lax.dot_general(half, x, (((1,), (1,)), ((), ())), **FULL) - diag
        x_ref[...] = x - nn((phi * error).astype(jnp.bfloat16), x.astype(jnp.bfloat16))
        return state[0] + 1, jnp.sum(error * error)

    _, size = lax.while_loop(more, refine, (0, jnp.float32(1.0)))
    inv_ref[...] = x_ref[...] * d_row

    @pl.when(jnp.logical_not(size < 1e-6))
    def _():
        x_ref[...] = diag
        s_ref[...] = scaled
        index = lax.broadcasted_iota(jnp.int32, (PANEL, 1), 0)
        lane = lax.broadcasted_iota(jnp.int32, (1, PANEL), 1)

        def eliminate(j, carry):
            s = s_ref[...]
            s_row = s_ref[pl.ds(j, 1), :]
            x_row = x_ref[pl.ds(j, 1), :]
            pivot = jnp.sum(jnp.where(lane == j, s_row, 0.0), 1, keepdims=True)
            column = jnp.sum(jnp.where(lane == j, s, 0.0), 1, keepdims=True)
            below = jnp.where(index > j, column / pivot, 0.0)
            s_ref[...] = s - below * s_row
            x = x_ref[...] - below * x_row
            x_ref[...] = jnp.where(index == j, x * lax.rsqrt(pivot), x)
            return carry

        lax.fori_loop(0, PANEL, eliminate, 0)
        inv_ref[...] = x_ref[...] * d_row


def factor_step(code):
    tile = lambda k: pl.BlockSpec((PANEL, LANES), lambda t: (0, k))
    return pl.pallas_call(
        factor_kernel,
        grid=(1,),
        in_specs=[
            pl.BlockSpec((PANEL, PANEL), lambda t: (0, (TILES + LOW + 1) // 2)),
            tile(GRAM_LOW),
            tile(TILES + LOW - 1),
        ],
        out_specs=pl.BlockSpec((PANEL, PANEL), lambda t: (0, 0)),
        out_shape=jax.ShapeDtypeStruct((PANEL, PANEL), jnp.float32),
        scratch_shapes=[pltpu.VMEM((PANEL, PANEL), jnp.float32)] * 2,
        compiler_params=pltpu.CompilerParams(vmem_limit_bytes=VMEM_LIMIT),
        name="factor",
    )(code, code, code)


def update_kernel(
    place, design, high, low, exponents, inverse_factor, panel, updated_ref, coupling_ref, q_ref
):
    t = pl.program_id(0)

    @pl.when(t == 0)
    def _():
        p_hi, p_lo = halves(panel[...])
        f_hi, f_lo = halves(inverse_factor[...])
        q_ref[...] = nt(p_hi, f_hi) + nt(p_hi, f_lo) + nt(p_lo, f_hi)

    @pl.when(t < place[1])
    def _():
        updated_ref[...] = design[...]
        coupling_ref[...] = jnp.zeros((PANEL, TILE), jnp.float32)

    @pl.when(t >= place[1])
    def _():
        f_hi, f_lo = halves(inverse_factor[...])
        low_bits = unsigned(low[...]) >> (8 * lax.rem(t, 2))
        exps = unsigned(exponents[...])
        left = decode(high[:, tile_of(0)], low_bits, 0, exps, 2 * t)
        right = decode(high[:, tile_of(1)], low_bits, 4, exps, 2 * t + 1)
        w_hi, w_lo = halves(jnp.concatenate([left, right], 1))
        coupling = nn(f_hi, w_hi) + nn(f_hi, w_lo) + nn(f_lo, w_hi)
        coupling_ref[...] = coupling
        q_hi, q_lo = halves(q_ref[...])
        c_hi, c_lo = halves(coupling)
        updated_ref[...] = design[...] - (nn(q_hi, c_hi) + nn(q_hi, c_lo) + nn(q_lo, c_hi))

    @pl.when(t == place[1])
    def _():
        updated_ref[...] = q_ref[...]


def update_step(place, design, code, inverse_factor, panel):
    return pl.pallas_call(
        update_kernel,
        grid_spec=pltpu.PrefetchScalarGridSpec(
            num_scalar_prefetch=1,
            grid=(SLOTS,),
            in_specs=[
                pl.BlockSpec((ROWS, TILE), lambda t, s: (0, t)),
                pl.BlockSpec((PANEL, TILE), lambda t, s: (0, t)),
                pl.BlockSpec((PANEL, LANES), lambda t, s: (0, TILES + t // 2)),
                pl.BlockSpec((PANEL, LANES), lambda t, s: (0, TILES + LOW - 1)),
                pl.BlockSpec((PANEL, PANEL), lambda t, s: (0, 0)),
                pl.BlockSpec((ROWS, PANEL), lambda t, s: (0, 0)),
            ],
            out_specs=(
                pl.BlockSpec((ROWS, TILE), lambda t, s: (0, t)),
                pl.BlockSpec((PANEL, TILE), lambda t, s: (0, t)),
            ),
            scratch_shapes=[pltpu.VMEM((ROWS, PANEL), jnp.float32)],
        ),
        out_shape=(
            jax.ShapeDtypeStruct((ROWS, COLS), jnp.float32),
            jax.ShapeDtypeStruct((PANEL, COLS), jnp.float32),
        ),
        compiler_params=pltpu.CompilerParams(vmem_limit_bytes=VMEM_LIMIT),
        name="update",
    )(place, design, code, code, code, inverse_factor, panel)


def shards(env_desc, env_counts, reg_desc, sparse_desc, panel_block):
    core = lax.axis_index("env") % 2
    column_shard = lax.axis_index("sp")
    owner = panel_block // SLOTS

    gathered = lax.all_gather(sparse_desc, "env", axis=1, tiled=True)

    with jax.named_scope("panel_points"):
        mine = lax.dynamic_index_in_dim(sparse_desc, panel_block - owner * SLOTS, 0, keepdims=False)
        offered = jnp.broadcast_to(mine[None], (N_SP,) + mine.shape)
        offered = lax.all_to_all(offered, "sp", 0, 0)
        mine = lax.dynamic_index_in_dim(offered, owner, 0, keepdims=False)
        panel_points = lax.all_gather(mine, "env", axis=0, tiled=True)

    counts = env_counts[0]
    finish = jnp.cumsum(counts)
    starts = finish - counts
    inverse = 1.0 / counts.astype(jnp.float32)
    place = jnp.stack([core, panel_block - column_shard * SLOTS]).astype(jnp.int32)
    panel, panel_hi, panel_lo, gram, member = panel_step(
        panel_points, env_desc, reg_desc, starts[:, None], finish[:, None], inverse[None, :]
    )

    with jax.named_scope("gram"):
        pieces = gram.reshape(4, 2, 4, GRAM_ROWS, PANEL).transpose(2, 0, 1, 3, 4)
        pieces = pieces.reshape(2 * N_Z, GRAM_ROWS, PANEL)
        pieces = lax.all_to_all(pieces, "env", 0, 0)

    points = gathered.reshape(COLS, DESC)
    design, keep, send = design_step(
        place, points, env_desc, reg_desc, member, inverse[:, None], panel_hi, panel_lo
    )

    with jax.named_scope("product"):
        send, pieces = lax.optimization_barrier((send, pieces))
        code = code_step(keep, lax.ppermute(send, "env", CORE_SWAP))
        code = code.reshape(4, BLOCK, CODE)
        code = lax.all_to_all(code, "env", 0, 0, axis_index_groups=NEAR)
        code = sum_step(near_kernel, CODE + LANES, code.reshape(HALF, CODE), pieces)
        code = lax.all_gather(code, "env", axis=0, tiled=True, axis_index_groups=FAR)
        code = sum_step(far_kernel, WIDE, code)
        code = lax.all_gather(code, "env", axis=0, tiled=True, axis_index_groups=CHIPS)

    return update_step(place, design, code, factor_step(code), panel)


def solution(mesh):
    in_specs = (P("env", None), P("env", None), P("env", None), P("sp", "env", None), P())
    out_specs = (P("env", "sp"), P(None, "sp"))
    return jax.shard_map(shards, mesh=mesh, in_specs=in_specs, out_specs=out_specs, check_vma=False)
```

```python
import jax
import jax.numpy as jnp
from jax import lax
from jax.experimental import pallas as pl
from jax.experimental.pallas import tpu as pltpu
from jax.sharding import PartitionSpec as P

DESC = 1000
PANEL = 256
TILE = 256
N_Z = 16
N_SP = 16
CONF = 448
ENV = 1024
REG = 64
ROWS = CONF + REG
SLOTS = 5
COLS = SLOTS * PANEL
HALF = PANEL // 2
START = 0.95
BLOCK = HALF // 4
GRAM_ROWS = 8
LANES = 128
TILES = COLS // LANES
LOW = 3
CODE = (TILES + LOW) * LANES
FIXED = 524286.0
GRAM_FIXED = 8388606.0
WIDE = CODE + 3 * LANES
GRAM_LOW = TILES + LOW

cube_scale = 15.0 ** (-0.5)
dot_scale = DESC ** (-0.5)
VMEM_LIMIT = 40 * 1024 * 1024
DESIGN_VMEM = 60 * 1024 * 1024

NEAR = [[2 * (4 * j + r) + c for r in range(4)] for j in range(4) for c in range(2)]
FAR = [[2 * (4 * j + r) + c for j in range(4)] for r in range(4) for c in range(2)]
CHIPS = [[8 * j + i for i in range(8)] for j in range(4)]
CORE_SWAP = [(i, i ^ 1) for i in range(2 * N_Z)]


def nt(a, b):
    return lax.dot_general(a, b, (((1,), (1,)), ((), ())), preferred_element_type=jnp.float32)


def nn(a, b):
    return lax.dot_general(a, b, (((1,), (0,)), ((), ())), preferred_element_type=jnp.float32)


def halves(x):
    hi = x.astype(jnp.bfloat16)
    lo = (x - hi.astype(jnp.float32)).astype(jnp.bfloat16)
    return hi, lo


def cubed(product):
    scaled = product * dot_scale
    return scaled * scaled * scaled * cube_scale


def panel_kernel(points, env, reg, starts, finish, inverse, panel_ref, hi_ref, lo_ref, gram_ref, member_ref):
    position = lax.broadcasted_iota(jnp.int32, (CONF, ENV), 1)
    inside = (position >= starts[...]) & (position < finish[...])
    member = inside.astype(jnp.float32).astype(jnp.bfloat16)
    member_ref[...] = member
    pts = points[...]
    hi, lo = halves(cubed(nt(pts, env[...])))
    energy = (nt(hi, member) + nt(lo, member)) * inverse[...]
    panel_t = jnp.concatenate([energy, cubed(nt(pts, reg[...]))], 1)
    panel_ref[...] = panel_t.T
    hi, lo = halves(panel_t)
    hi_ref[...] = hi
    lo_ref[...] = lo
    gram_ref[...] = lax.dot_general(
        panel_t,
        panel_t,
        (((1,), (1,)), ((), ())),
        precision=lax.Precision.HIGHEST,
        preferred_element_type=jnp.float32,
    )


def panel_step(points, env, reg, starts, finish, inverse):
    return pl.pallas_call(
        panel_kernel,
        out_shape=(
            jax.ShapeDtypeStruct((ROWS, PANEL), jnp.float32),
            jax.ShapeDtypeStruct((PANEL, ROWS), jnp.bfloat16),
            jax.ShapeDtypeStruct((PANEL, ROWS), jnp.bfloat16),
            jax.ShapeDtypeStruct((PANEL, PANEL), jnp.float32),
            jax.ShapeDtypeStruct((CONF, ENV), jnp.bfloat16),
        ),
        compiler_params=pltpu.CompilerParams(vmem_limit_bytes=VMEM_LIMIT),
        name="panel",
    )(points, env, reg, starts, finish, inverse)


def design_kernel(
    place, points, env, reg, member, inverse, panel_hi, panel_lo, design_ref, keep_ref, send_ref, rows_ref, sem
):
    pts = points[...]
    hi, lo = halves(cubed(nt(env[...], pts)))
    weights = member[...]
    rows_ref[:CONF] = (nn(weights, hi) + nn(weights, lo)) * inverse[...]
    rows_ref[CONF:] = cubed(nt(reg[...], pts))
    leave = pltpu.make_async_copy(rows_ref, design_ref, sem)
    leave.start()
    hi, lo = halves(rows_ref[...])
    left = panel_hi[...]
    product = nn(left, hi) + nn(left, lo) + nn(panel_lo[...], hi)
    product = product.reshape(4, 2, BLOCK, COLS)
    first = place[0] == 0
    keep_ref[...] = jnp.where(first, product[:, 0], product[:, 1]).reshape(HALF, COLS)
    send_ref[...] = jnp.where(first, product[:, 1], product[:, 0]).reshape(HALF, COLS)
    leave.wait()


def design_step(place, points, env, reg, member, inverse, panel_hi, panel_lo):
    half = pl.BlockSpec((HALF, COLS), lambda t, s: (0, 0))
    arrays = (points, env, reg, member, inverse, panel_hi, panel_lo)
    return pl.pallas_call(
        design_kernel,
        grid_spec=pltpu.PrefetchScalarGridSpec(
            num_scalar_prefetch=1,
            grid=(1,),
            in_specs=[pl.BlockSpec(a.shape, lambda t, s: (0, 0)) for a in arrays],
            out_specs=(pl.BlockSpec(memory_space=pl.ANY), half, half),
            scratch_shapes=[pltpu.VMEM((ROWS, COLS), jnp.float32), pltpu.SemaphoreType.DMA],
        ),
        out_shape=(
            jax.ShapeDtypeStruct((ROWS, COLS), jnp.float32),
            jax.ShapeDtypeStruct((HALF, COLS), jnp.float32),
            jax.ShapeDtypeStruct((HALF, COLS), jnp.float32),
        ),
        compiler_params=pltpu.CompilerParams(vmem_limit_bytes=DESIGN_VMEM),
        cost_estimate=pl.CostEstimate(flops=7 * 10**9, bytes_accessed=9 * 10**6, transcendentals=0),
        name="design",
    )(place, *arrays)


def tile_of(t):
    return slice(t * LANES, (t + 1) * LANES)


def fixed_point(x, limit):
    largest = jnp.maximum(jnp.max(jnp.abs(x), 1, keepdims=True), 1e-30)
    exponent = jnp.minimum(jnp.ceil(jnp.log2(largest) + 1e-4), 127.0)
    scaled = jnp.clip(x * (jnp.exp2(-exponent) * limit), -limit, limit)
    return jnp.where(scaled < 0, scaled - 0.5, scaled + 0.5).astype(jnp.int32), exponent.astype(jnp.int32) + 128


def encode(tiles, code_ref):
    rows = code_ref.shape[0]
    lane = lax.broadcasted_iota(jnp.int32, (rows, LANES), 1)
    low = [jnp.zeros((rows, LANES), jnp.int32) for _ in range(LOW)]
    for t, x in enumerate(tiles):
        rounded, exponent = fixed_point(x, FIXED)
        code_ref[:, tile_of(t)] = (rounded >> 4).astype(jnp.int16)
        low[t // 4] = low[t // 4] + ((rounded & 15) << (4 * (t % 4)))
        low[-1] = low[-1] + jnp.where(lane == t, exponent << 8, 0)
    return low, lane


def unsigned(code):
    return code.astype(jnp.int32) + 32768


def unit(exponents, t, limit):
    lane = lax.broadcasted_iota(jnp.int32, exponents.shape, 1)
    exponent = jnp.sum(jnp.where(lane == t, (exponents >> 8) - 128, 0).astype(jnp.float32), 1, keepdims=True)
    return jnp.exp2(exponent) * (1.0 / limit)


def decode(high, low, shift, exponents, t):
    number = high.astype(jnp.int32) * 16 + ((low >> shift) & 15)
    return number.astype(jnp.float32) * unit(exponents, t, FIXED)


def code_kernel(kept, received, code_ref, keep, sem):
    bring = pltpu.make_async_copy(kept, keep, sem)
    bring.start()
    bring.wait()
    low, _ = encode([keep[:, tile_of(t)] + received[:, tile_of(t)] for t in range(TILES)], code_ref)
    for k in range(LOW):
        code_ref[:, tile_of(TILES + k)] = (low[k] - 32768).astype(jnp.int16)


def quarter_sums(code):
    low = [unsigned(code[:, tile_of(TILES + k)]) for k in range(LOW)]
    tiles = []
    for t in range(TILES):
        x = decode(code[:, tile_of(t)], low[t // 4], 4 * (t % 4), low[-1], t)
        tiles.append(jnp.sum(x.reshape(4, BLOCK, LANES), 0))
    return tiles


def near_kernel(code, pieces, code_ref):
    out, lane = encode(quarter_sums(code), code_ref)
    rest = jnp.zeros((BLOCK - GRAM_ROWS, LANES), jnp.int32)
    gram = jnp.sum(pieces[...], 0)
    groups = []
    gram_low = jnp.zeros((GRAM_ROWS, LANES), jnp.int32)
    for g in range(2):
        rounded, exponent = fixed_point(gram[:, tile_of(g)], GRAM_FIXED)
        groups.append(rounded >> 8)
        gram_low = gram_low + ((rounded & 255) << (8 * g))
        exponents = jnp.where(lane[:GRAM_ROWS] == TILES + g, exponent << 8, 0)
        out[-1] = out[-1] + jnp.concatenate([exponents, rest], 0)
    for k in range(LOW):
        code_ref[:, tile_of(TILES + k)] = (out[k] - 32768).astype(jnp.int16)
    groups = [gram_low - 32768] + groups + [rest[:GRAM_ROWS]]
    code_ref[:, tile_of(GRAM_LOW)] = jnp.concatenate(groups, 0).astype(jnp.int16)


def far_kernel(code, code_ref):
    out, lane = encode(quarter_sums(code), code_ref)

    def gram_rows(x, k):
        first = [BLOCK * j + GRAM_ROWS * k for j in range(4)]
        return jnp.concatenate([x[i : i + GRAM_ROWS] for i in first], 0)

    for k in range(3):
        tile = code[:, tile_of(GRAM_LOW)].astype(jnp.int32)
        code_ref[:, tile_of(GRAM_LOW + k)] = gram_rows(tile, k).astype(jnp.int16)
    exponents = gram_rows((unsigned(code[:, tile_of(TILES + LOW - 1)]) >> 8) << 8, 0)
    out[-1] = out[-1] + jnp.where((lane == TILES) | (lane == TILES + 1), exponents, 0)
    for k in range(LOW):
        code_ref[:, tile_of(TILES + k)] = (out[k] - 32768).astype(jnp.int16)


def code_step(keep, received):
    vmem = pl.BlockSpec(memory_space=pltpu.VMEM)
    return pl.pallas_call(
        code_kernel,
        in_specs=[pl.BlockSpec(memory_space=pl.ANY), vmem],
        out_specs=vmem,
        out_shape=jax.ShapeDtypeStruct((HALF, CODE), jnp.int16),
        scratch_shapes=[pltpu.VMEM((HALF, COLS), jnp.float32), pltpu.SemaphoreType.DMA],
        compiler_params=pltpu.CompilerParams(vmem_limit_bytes=VMEM_LIMIT),
        name="code",
    )(keep, received)


def sum_step(kernel, width, *arrays):
    vmem = pl.BlockSpec(memory_space=pltpu.VMEM)
    return pl.pallas_call(
        kernel,
        in_specs=[vmem] * len(arrays),
        out_specs=vmem,
        out_shape=jax.ShapeDtypeStruct((BLOCK, width), jnp.int16),
        compiler_params=pltpu.CompilerParams(vmem_limit_bytes=VMEM_LIMIT),
        name="sum",
    )(*arrays)


FULL = dict(precision=lax.Precision.HIGHEST, preferred_element_type=jnp.float32)


def factor_kernel(high, low, exponents, inv_ref, x_ref, s_ref):
    row = lax.broadcasted_iota(jnp.int32, (PANEL, PANEL), 0)
    col = lax.broadcasted_iota(jnp.int32, (PANEL, PANEL), 1)
    diag = (row == col).astype(jnp.float32)
    phi = jnp.where(row > col, 1.0, 0.5 * diag)
    low_bits = unsigned(low[...])
    exps = unsigned(exponents[...])

    def gram_tile(k):
        number = high[:, tile_of(k)].astype(jnp.int32) * 256 + ((low_bits >> (8 * k)) & 255)
        return number.astype(jnp.float32) * unit(exps, TILES + k, GRAM_FIXED)

    g = jnp.concatenate([gram_tile(0), gram_tile(1)], 1)
    g = jnp.where(row >= col, g, g.T)
    on_diag = g * diag
    d_row = lax.rsqrt(jnp.sum(on_diag, 0, keepdims=True))
    d_col = lax.rsqrt(jnp.sum(on_diag, 1, keepdims=True))
    scaled = g * d_row * d_col
    x = START * (diag - phi * (START * START * scaled - diag))
    low = scaled.astype(jnp.bfloat16)
    for _ in range(2):
        x_low = x.astype(jnp.bfloat16)
        error = nt(nn(x_low, low).astype(jnp.bfloat16), x_low) - diag
        x = x - nn((phi * error).astype(jnp.bfloat16), x_low)
    x_ref[...] = x
    s_ref[...] = scaled

    def more(state):
        step, size = state
        return (step < 12) & (size >= 1e-6) & (size < 1e6)

    def refine(state):
        x = x_ref[...]
        half = lax.dot_general(x, s_ref[...], (((1,), (0,)), ((), ())), **FULL)
        error = lax.dot_general(half, x, (((1,), (1,)), ((), ())), **FULL) - diag
        x_ref[...] = x - nn((phi * error).astype(jnp.bfloat16), x.astype(jnp.bfloat16))
        return state[0] + 1, jnp.sum(error * error)

    _, size = lax.while_loop(more, refine, (0, jnp.float32(1.0)))
    inv_ref[...] = x_ref[...] * d_row

    @pl.when(jnp.logical_not(size < 1e-6))
    def _():
        x_ref[...] = diag
        s_ref[...] = scaled
        index = lax.broadcasted_iota(jnp.int32, (PANEL, 1), 0)
        lane = lax.broadcasted_iota(jnp.int32, (1, PANEL), 1)

        def eliminate(j, carry):
            s = s_ref[...]
            s_row = s_ref[pl.ds(j, 1), :]
            x_row = x_ref[pl.ds(j, 1), :]
            pivot = jnp.sum(jnp.where(lane == j, s_row, 0.0), 1, keepdims=True)
            column = jnp.sum(jnp.where(lane == j, s, 0.0), 1, keepdims=True)
            below = jnp.where(index > j, column / pivot, 0.0)
            s_ref[...] = s - below * s_row
            x = x_ref[...] - below * x_row
            x_ref[...] = jnp.where(index == j, x * lax.rsqrt(pivot), x)
            return carry

        lax.fori_loop(0, PANEL, eliminate, 0)
        inv_ref[...] = x_ref[...] * d_row


def factor_step(code):
    tile = lambda k: pl.BlockSpec((PANEL, LANES), lambda t: (0, k))
    return pl.pallas_call(
        factor_kernel,
        grid=(1,),
        in_specs=[
            pl.BlockSpec((PANEL, PANEL), lambda t: (0, (TILES + LOW + 1) // 2)),
            tile(GRAM_LOW),
            tile(TILES + LOW - 1),
        ],
        out_specs=pl.BlockSpec((PANEL, PANEL), lambda t: (0, 0)),
        out_shape=jax.ShapeDtypeStruct((PANEL, PANEL), jnp.float32),
        scratch_shapes=[pltpu.VMEM((PANEL, PANEL), jnp.float32)] * 2,
        compiler_params=pltpu.CompilerParams(vmem_limit_bytes=VMEM_LIMIT),
        name="factor",
    )(code, code, code)


def update_kernel(
    place, design, high, low, exponents, inverse_factor, panel, updated_ref, coupling_ref, q_ref
):
    t = pl.program_id(0)

    @pl.when(t == 0)
    def _():
        p_hi, p_lo = halves(panel[...])
        f_hi, f_lo = halves(inverse_factor[...])
        q_ref[...] = nt(p_hi, f_hi) + nt(p_hi, f_lo) + nt(p_lo, f_hi)

    @pl.when(t < place[1])
    def _():
        updated_ref[...] = design[...]
        coupling_ref[...] = jnp.zeros((PANEL, TILE), jnp.float32)

    @pl.when(t >= place[1])
    def _():
        f_hi, f_lo = halves(inverse_factor[...])
        low_bits = unsigned(low[...]) >> (8 * lax.rem(t, 2))
        exps = unsigned(exponents[...])
        left = decode(high[:, tile_of(0)], low_bits, 0, exps, 2 * t)
        right = decode(high[:, tile_of(1)], low_bits, 4, exps, 2 * t + 1)
        w_hi, w_lo = halves(jnp.concatenate([left, right], 1))
        coupling = nn(f_hi, w_hi) + nn(f_hi, w_lo) + nn(f_lo, w_hi)
        coupling_ref[...] = coupling
        q_hi, q_lo = halves(q_ref[...])
        c_hi, c_lo = halves(coupling)
        updated_ref[...] = design[...] - (nn(q_hi, c_hi) + nn(q_hi, c_lo) + nn(q_lo, c_hi))

    @pl.when(t == place[1])
    def _():
        updated_ref[...] = q_ref[...]


def update_step(place, design, code, inverse_factor, panel):
    return pl.pallas_call(
        update_kernel,
        grid_spec=pltpu.PrefetchScalarGridSpec(
            num_scalar_prefetch=1,
            grid=(SLOTS,),
            in_specs=[
                pl.BlockSpec((ROWS, TILE), lambda t, s: (0, t)),
                pl.BlockSpec((PANEL, TILE), lambda t, s: (0, t)),
                pl.BlockSpec((PANEL, LANES), lambda t, s: (0, TILES + t // 2)),
                pl.BlockSpec((PANEL, LANES), lambda t, s: (0, TILES + LOW - 1)),
                pl.BlockSpec((PANEL, PANEL), lambda t, s: (0, 0)),
                pl.BlockSpec((ROWS, PANEL), lambda t, s: (0, 0)),
            ],
            out_specs=(
                pl.BlockSpec((ROWS, TILE), lambda t, s: (0, t)),
                pl.BlockSpec((PANEL, TILE), lambda t, s: (0, t)),
            ),
            scratch_shapes=[pltpu.VMEM((ROWS, PANEL), jnp.float32)],
        ),
        out_shape=(
            jax.ShapeDtypeStruct((ROWS, COLS), jnp.float32),
            jax.ShapeDtypeStruct((PANEL, COLS), jnp.float32),
        ),
        compiler_params=pltpu.CompilerParams(vmem_limit_bytes=VMEM_LIMIT),
        name="update",
    )(place, design, code, code, code, inverse_factor, panel)


def shards(env_desc, env_counts, reg_desc, sparse_desc, panel_block):
    core = lax.axis_index("env") % 2
    column_shard = lax.axis_index("sp")
    owner = panel_block // SLOTS

    gathered = lax.all_gather(sparse_desc, "env", axis=1, tiled=True)

    with jax.named_scope("panel_points"):
        mine = lax.dynamic_index_in_dim(sparse_desc, panel_block - owner * SLOTS, 0, keepdims=False)
        offered = jnp.broadcast_to(mine[None], (N_SP,) + mine.shape)
        offered = lax.all_to_all(offered, "sp", 0, 0)
        mine = lax.dynamic_index_in_dim(offered, owner, 0, keepdims=False)
        panel_points = lax.all_gather(mine, "env", axis=0, tiled=True)

    counts = env_counts[0]
    finish = jnp.cumsum(counts)
    starts = finish - counts
    inverse = 1.0 / counts.astype(jnp.float32)
    place = jnp.stack([core, panel_block - column_shard * SLOTS]).astype(jnp.int32)
    panel, panel_hi, panel_lo, gram, member = panel_step(
        panel_points, env_desc, reg_desc, starts[:, None], finish[:, None], inverse[None, :]
    )

    with jax.named_scope("gram"):
        pieces = gram.reshape(4, 2, 4, GRAM_ROWS, PANEL).transpose(2, 0, 1, 3, 4)
        pieces = pieces.reshape(2 * N_Z, GRAM_ROWS, PANEL)
        pieces = lax.all_to_all(pieces, "env", 0, 0)

    points = gathered.reshape(COLS, DESC)
    design, keep, send = design_step(
        place, points, env_desc, reg_desc, member, inverse[:, None], panel_hi, panel_lo
    )

    with jax.named_scope("product"):
        send, pieces = lax.optimization_barrier((send, pieces))
        code = code_step(keep, lax.ppermute(send, "env", CORE_SWAP))
        code = code.reshape(4, BLOCK, CODE)
        code = lax.all_to_all(code, "env", 0, 0, axis_index_groups=NEAR)
        code = sum_step(near_kernel, CODE + LANES, code.reshape(HALF, CODE), pieces)
        code = lax.all_gather(code, "env", axis=0, tiled=True, axis_index_groups=FAR)
        code = sum_step(far_kernel, WIDE, code)
        code = lax.all_gather(code, "env", axis=0, tiled=True, axis_index_groups=CHIPS)

    return update_step(place, design, code, factor_step(code), panel)


def solution(mesh):
    in_specs = (P("env", None), P("env", None), P("env", None), P("sp", "env", None), P())
    out_specs = (P("env", "sp"), P(None, "sp"))
    return jax.shard_map(shards, mesh=mesh, in_specs=in_specs, out_specs=out_specs, check_vma=False)
```
